512 devices in a mesh: ctx: 32 (over x, y), tp: 16 (over z, core).
Axes of the slice: x: 4, y: 8, z: 8, core: 2. Of those that a mesh axis runs over, the one named last changes fastest.
Arguments:
- hidden: bfloat16 [6144, 16384], P(('ctx', 'tp')), may hold values from -32 to 32
- query_weight: bfloat16 [16384, 2048], P('ctx', 'tp'), may hold values from -0.046875 to 0.046875
- kv_weight: bfloat16 [16384, 256], P('tp'), may hold values from -0.046875 to 0.046875
Outputs:
- context_out: bfloat16 [6144, 2048], P('ctx', 'tp')
The draws below stay inside these ranges and needn't reach their ends.
All inputs are finite; a program needn't handle non-finite values.
Results may differ from the reference program's by a relative error of at most 0.0315.
The reference program's roundings to bfloat16 on the way count: a program that leaves them out, or rounds other values in their place, can miss the bound.
Values may be sent and summed in bfloat16 or wider, within the bound.
No kernel may reach another device: no remote copies, remote signals or barrier semaphores. Data moves between devices by JAX's collectives and lax.ppermute only.
A program may use at most 64 MiB of HBM per device.

```python
import jax
import jax.numpy as jnp
from jax import lax

D = 16384
HD = 128
QH = 16
TOKENS = 6144


def draw_hidden(key, part):
    key = jax.random.fold_in(key, 11)
    first_key = jax.random.fold_in(key, 0)
    normal = jax.random.normal(first_key, (TOKENS, D), jnp.float32)
    return jnp.clip(normal, -4.0, 4.0).astype(jnp.bfloat16)


def levels(stream_key, shape, cuts, smallest, high):
    def one(axis_at, parts):
        heights = jax.random.uniform(jax.random.fold_in(jax.random.fold_in(stream_key, 6), axis_at), (parts,), jnp.float32, smallest / len(cuts), high / len(cuts))
        return jnp.repeat(jnp.exp(heights), shape[axis_at] // parts).reshape((-1,) + (1,) * (len(shape) - axis_at - 1))

    gain = one(*cuts[0])
    for cut in cuts[1:]:
        gain = gain * one(*cut)
    return gain


def scatter_about(stream_key, extent, deviation, limit, cuts=(), kind=jnp.bfloat16):
    loudness = levels(stream_key, extent, cuts, -0.22, 0.18) if cuts else 1.0
    array = jax.random.normal(stream_key, extent, jnp.float32) * deviation * loudness
    return jnp.minimum(jnp.maximum(array, -limit), limit).astype(kind)


def setup_inputs(seed: int = 0) -> dict:
    arg_keys = jax.random.split(jax.random.key(seed), 4)
    hidden = draw_hidden(jax.random.fold_in(arg_keys[3], 71), 0)
    query_weight = scatter_about(arg_keys[1], (D, QH * HD), D ** -0.5, 0.046875, ((0, 32), (1, 16)))
    kv_weight = scatter_about(arg_keys[2], (D, 2 * HD), D ** -0.5, 0.046875, ((0, 16),))
    return dict(hidden=hidden, query_weight=query_weight, kv_weight=kv_weight)


def rotate(field, positions):
    half_width = field.shape[1] // 2
    exponent = jnp.arange(half_width, dtype=jnp.float32) * (2.0 / field.shape[1])
    frequency = jnp.power(jnp.float32(500000.0), -exponent)
    angles = positions.astype(jnp.float32)[:, None] * frequency[None, :]
    cosine = jnp.cos(angles)
    sine = jnp.sin(angles)
    first_half = field[:, :half_width]
    second_half = field[:, half_width:]
    return jnp.concatenate([first_half * cosine - second_half * sine, second_half * cosine + first_half * sine], axis=1)


def reference(hidden, query_weight, kv_weight):
    positions = jnp.arange(TOKENS, dtype=jnp.int32)
    kv_proj = jnp.dot(hidden, kv_weight, preferred_element_type=jnp.float32)
    key_rows = rotate(kv_proj[:, :HD], positions).astype(jnp.bfloat16)
    value_rows = kv_proj[:, HD:].astype(jnp.bfloat16)
    queries = jnp.dot(hidden, query_weight, preferred_element_type=jnp.float32)
    allowed = positions[:, None] >= positions[None, :]

    def single_head(head_index):
        start = (head_index * HD).astype(jnp.int32)
        head_query = rotate(lax.dynamic_slice_in_dim(queries, start, HD, 1), positions).astype(jnp.bfloat16)
        scores = jnp.dot(head_query, key_rows.T, preferred_element_type=jnp.float32) * (HD ** -0.5)
        scores = jnp.where(allowed, scores, -jnp.inf)
        maxima = jnp.max(scores, axis=1, keepdims=True)
        expo = jnp.exp(scores - maxima)
        totals = jnp.sum(expo, axis=1, keepdims=True)
        weights = expo.astype(jnp.bfloat16)
        output = jnp.dot(weights, value_rows, preferred_element_type=jnp.float32) / totals
        return output.astype(jnp.bfloat16)

    stacked = lax.map(single_head, jnp.arange(QH, dtype=jnp.int32))
    return jnp.transpose(stacked, (1, 0, 2)).reshape(TOKENS, QH * HD)
```

```python
import math

import jax
import jax.numpy as jnp
from jax import lax
from jax.experimental import pallas as pl
from jax.experimental.pallas import tpu as pltpu
from jax.sharding import Mesh
from jax.sharding import PartitionSpec as P

HD = 128
CTX = ("x", "yh", "yl")
TP = ("z", "core")
AXES = CTX + TP
KEY_TILE = 768


def fine_mesh(mesh):
    return Mesh(mesh.devices.reshape(4, 2, 4, 8, 2), AXES)


def angles_of(positions):
    half = HD // 2
    exponent = jnp.arange(half, dtype=jnp.float32) * (2.0 / HD)
    frequency = jnp.power(jnp.float32(500000.0), -exponent)
    angles = positions.astype(jnp.float32)[:, None] * frequency[None, :]
    return jnp.cos(angles), jnp.sin(angles)


def rotate(field, cosine, sine):
    half = HD // 2
    first, second = field[:, :half], field[:, half:]
    return jnp.concatenate(
        [first * cosine - second * sine, second * cosine + first * sine], axis=1
    )


def broadcast_gather(x, axis):
    n = lax.axis_size(axis)
    return lax.all_to_all(
        jnp.broadcast_to(x[None], (n,) + x.shape), axis, 0, 0, tiled=True
    )


def project_kernel(info_ref, h_ref, *refs):
    w_refs, o_ref, h_buf, w_buf, sems = refs[:4], *refs[4:]
    x = info_ref[0]
    copies = []
    for n in range(4):
        at = pl.multiple_of(lax.rem(x + 4 - n, 4) * 2048, 2048)
        copies.append(
            (
                pltpu.make_async_copy(h_ref.at[:, pl.ds(at, 2048)], h_buf.at[n], sems.at[n, 0]),
                pltpu.make_async_copy(w_refs[n], w_buf.at[n], sems.at[n, 1]),
            )
        )
        for copy in copies[n]:
            copy.start()
    total = None
    for n in range(4):
        for copy in copies[n]:
            copy.wait()
        term = jnp.dot(h_buf[n], w_buf[n], preferred_element_type=jnp.float32)
        total = term if total is None else total + term
    for part in range(16):
        for sel in range(2):
            at = part * 24 + sel * 12
            o_ref[sel, part * 12 : part * 12 + 12, :] = total[at : at + 12]


def attend_kernel(info_ref, q_ref, cos_ref, sin_ref, *refs):
    mine, near_ref, far_ref, o_ref, buf, s_ref, sems = refs[:4], *refs[4:]
    rows = q_ref.shape[0]
    x, y, core = info_ref[0], info_ref[1], info_ref[2]
    size = near_ref.shape[0]
    own = (y * rows) // KEY_TILE
    full = own + x * (size // KEY_TILE)

    def copies(i):
        other = near_ref if i == 0 else far_ref.at[pl.ds((i - 1) * size, size)]
        return [
            pltpu.make_async_copy(mine[i], buf.at[i, core], sems.at[i, 0]),
            pltpu.make_async_copy(other, buf.at[i, 1 - core], sems.at[i, 1]),
        ]

    for i in range(4):

        @pl.when(x >= i)
        def _(i=i):
            for copy in copies(i):
                copy.start()

    sums = q_ref[...]
    q = sums * cos_ref[...] + pltpu.roll(sums, HD // 2, 1) * sin_ref[...]
    q = q.astype(jnp.bfloat16)

    def where(j):
        back = jnp.where(j < own, 0, (j - own) // (size // KEY_TILE) + 1)
        first = jnp.where(j < own, 0, lax.rem(j - own, size // KEY_TILE)) * KEY_TILE
        return back, pl.ds(pl.multiple_of(first, KEY_TILE), KEY_TILE)

    def lanes(v, op):
        out = v[:, :HD]
        for i in range(1, v.shape[1] // HD):
            out = op(out, v[:, i * HD : (i + 1) * HD])
        return out

    def scores(k):
        return lax.dot_general(
            q, k, (((1,), (1,)), ((), ())), preferred_element_type=jnp.float32
        )

    for copy in copies(0):
        copy.wait()
    at = pl.multiple_of(own * KEY_TILE, KEY_TILE)
    s = scores(buf[0, 0, pl.ds(at, KEY_TILE), :])
    qp = y * rows + lax.broadcasted_iota(jnp.int32, s.shape, 0)
    kp = at + lax.broadcasted_iota(jnp.int32, s.shape, 1)
    s = jnp.where(qp >= kp, s, -jnp.inf)
    s_ref[full] = s
    top = lanes(s, jnp.maximum)
    for i in range(1, 4):

        @pl.when(x >= i)
        def _(i=i):
            for copy in copies(i):
                copy.wait()

    def first_pass(j, top):
        back, at = where(j)
        s = scores(buf[back, 0, at, :])
        s_ref[j] = s
        return jnp.maximum(top, lanes(s, jnp.maximum))

    top = jnp.max(lax.fori_loop(0, full, first_pass, top), axis=1, keepdims=True)
    scale = HD**-0.5 * math.log2(math.e)

    def weigh(s, v, state):
        tot, acc = state
        e = jnp.exp2((s - top) * scale)
        return tot + lanes(e, jnp.add), acc + jnp.dot(
            e.astype(jnp.bfloat16), v, preferred_element_type=jnp.float32
        )

    def second_pass(j, state):
        back, at = where(j)
        return weigh(s_ref[j], buf[back, 1, at, :], state)

    zero = jnp.zeros((rows, HD), jnp.float32)
    state = weigh(s_ref[full], buf[0, 1, pl.ds(at, KEY_TILE), :], (zero, zero))
    tot, acc = lax.fori_loop(0, full, second_pass, state)
    o_ref[...] = (acc / jnp.sum(tot, axis=1, keepdims=True)).astype(o_ref.dtype)


def project(info, h, pieces):
    m, depth = h.shape
    hbm = pl.BlockSpec(memory_space=pl.ANY)
    return pl.pallas_call(
        project_kernel,
        in_specs=[pl.BlockSpec(memory_space=pltpu.SMEM)] + [hbm] * 5,
        out_specs=pl.BlockSpec(memory_space=pltpu.VMEM),
        out_shape=jax.ShapeDtypeStruct((2, m // 2, HD), jnp.float32),
        scratch_shapes=[
            pltpu.VMEM((4, m, depth // 4), jnp.bfloat16),
            pltpu.VMEM((4, depth // 4, HD), jnp.bfloat16),
            pltpu.SemaphoreType.DMA((4, 2)),
        ],
        compiler_params=pltpu.CompilerParams(vmem_limit_bytes=48 * 2**20),
        cost_estimate=pl.CostEstimate(
            flops=2 * m * depth * HD, bytes_accessed=2 * depth * (m + HD), transcendentals=0
        ),
        name="project",
    )(info, h, *pieces)


def attend(info, sums, cosine, sine, mine, other):
    vm = pl.BlockSpec(memory_space=pltpu.VMEM)
    return pl.pallas_call(
        attend_kernel,
        in_specs=[pl.BlockSpec(memory_space=pltpu.SMEM), vm, vm, vm]
        + [pl.BlockSpec(memory_space=pl.ANY)] * 6,
        out_specs=vm,
        out_shape=jax.ShapeDtypeStruct(sums.shape, jnp.bfloat16),
        scratch_shapes=[
            pltpu.VMEM((4, 2, 1536, HD), jnp.bfloat16),
            pltpu.VMEM((6144 // KEY_TILE, 192, KEY_TILE), jnp.float32),
            pltpu.SemaphoreType.DMA((4, 2)),
        ],
        compiler_params=pltpu.CompilerParams(vmem_limit_bytes=40 * 2**20),
        cost_estimate=pl.CostEstimate(
            flops=4 * 192 * 6144 * HD,
            bytes_accessed=4 * 6144 * HD,
            transcendentals=192 * 6144,
        ),
        name="attend",
    )(info, sums, cosine, sine, *mine, *other)


def shift(v, axis, by):
    n = lax.axis_size(axis)
    return lax.ppermute(v, axis, [(i, (i + by) % n) for i in range(n)])


def shift_up(v, axis, by):
    n = lax.axis_size(axis)
    return lax.ppermute(v, axis, [(i, i + by) for i in range(n - by)])


def swap(v, axis):
    return lax.ppermute(v, axis, [(0, 1), (1, 0)])


def body(hidden, query_weight, kv_weight):
    x, yh, yl, z, core = (lax.axis_index(a) for a in AXES)
    y = yh * 4 + yl
    base = (x * 8 + y) * 192
    info = jnp.stack([x, y, core])
    tie = lax.optimization_barrier

    w = lax.all_gather(query_weight, "yl", axis=0, tiled=True)

    hs = hidden.reshape(12, 16, 1024).transpose(1, 0, 2)
    hs, hidden = tie((hs, hidden))
    hs = lax.all_to_all(hs, TP, 0, 0, tiled=True).reshape(192, 1024)

    parts = [hidden[:, i * 2048 : (i + 1) * 2048] for i in range(8)]
    halves = [jnp.concatenate(parts[i::2], axis=1) for i in range(2)]
    keep = jnp.where(yh == 0, halves[0], halves[1])
    come = swap(jnp.where(yh == 0, halves[1], halves[0]), "yh")
    h = jnp.where(
        yh == 0, jnp.concatenate([keep, come], 0), jnp.concatenate([come, keep], 0)
    )
    part = jnp.dot(hs, kv_weight, preferred_element_type=jnp.float32)
    part = part.reshape(8, 24, 2, HD).transpose(0, 2, 1, 3).reshape(16, 24, HD)
    h, w, part = tie((h, w, part))
    h = lax.all_gather(h, TP, axis=0, tiled=True)

    part = lax.all_to_all(part, TP, 0, 0, tiled=True)
    up, down = shift(w, "x", 1), shift(w, "x", -1)
    rows = jnp.sum(part, axis=0)
    cosine, sine = angles_of(base + z * 24 + jnp.arange(24, dtype=jnp.int32))
    rows = jnp.where(core == 0, rotate(rows, cosine, sine), rows).astype(jnp.bfloat16)
    rows, up, down = tie((rows, up, down))
    rows = broadcast_gather(rows, ("yh", "yl", "z")).reshape(1536, HD)
    cross = [shift(up[:1024], "x", 1), shift(down[1024:], "x", -1)]
    rows, cross = tie((rows, cross))
    mine = [rows] + [shift_up(rows, "x", d) for d in (1, 2, 3)]

    sums = project(info, h, (w, up, jnp.concatenate(cross, axis=0), down))
    come, sums = tie((mine[1:], sums))
    other = [swap(rows, "core"), swap(jnp.concatenate(come, axis=0), "core")]
    keep = jnp.where(yh == 0, sums[0], sums[1])
    come = swap(jnp.where(yh == 0, sums[1], sums[0]), "yh")
    cosine, sine = angles_of(base + jnp.arange(192, dtype=jnp.int32))
    cosine = jnp.concatenate([cosine, cosine], axis=1)
    sine = jnp.concatenate([-sine, sine], axis=1)
    return attend(info, keep + come, cosine, sine, mine, other)


def solution(mesh):
    in_specs = (P(AXES, None), P(CTX, TP), P(TP, None))
    out_specs = P(CTX, TP)
    return jax.shard_map(
        body, mesh=fine_mesh(mesh), in_specs=in_specs, out_specs=out_specs, check_vma=False
    )
```

```python
import math

import jax
import jax.numpy as jnp
from jax import lax
from jax.experimental import pallas as pl
from jax.experimental.pallas import tpu as pltpu
from jax.sharding import Mesh
from jax.sharding import PartitionSpec as P

HD = 128
CTX = ("x", "yh", "yl")
TP = ("z", "core")
AXES = CTX + TP


def fine_mesh(mesh):
    return Mesh(mesh.devices.reshape(4, 2, 4, 8, 2), AXES)


def angles_of(positions):
    half = HD // 2
    exponent = jnp.arange(half, dtype=jnp.float32) * (2.0 / HD)
    frequency = jnp.power(jnp.float32(500000.0), -exponent)
    angles = positions.astype(jnp.float32)[:, None] * frequency[None, :]
    return jnp.cos(angles), jnp.sin(angles)


def rotate(field, cosine, sine):
    half = HD // 2
    first, second = field[:, :half], field[:, half:]
    return jnp.concatenate(
        [first * cosine - second * sine, second * cosine + first * sine], axis=1
    )


def broadcast_gather(x, axis):
    n = lax.axis_size(axis)
    return lax.all_to_all(
        jnp.broadcast_to(x[None], (n,) + x.shape), axis, 0, 0, tiled=True
    )


def project_kernel(info_ref, h_ref, *refs):
    w_refs, o_ref, h_buf, w_buf, sems = refs[:4], *refs[4:]
    x = info_ref[0]
    copies = []
    for n in range(4):
        at = pl.multiple_of(lax.rem(x + 4 - n, 4) * 2048, 2048)
        copies.append(
            (
                pltpu.make_async_copy(h_ref.at[:, pl.ds(at, 2048)], h_buf.at[n], sems.at[n, 0]),
                pltpu.make_async_copy(w_refs[n], w_buf.at[n], sems.at[n, 1]),
            )
        )
        for copy in copies[n]:
            copy.start()
    total = None
    for n in range(4):
        for copy in copies[n]:
            copy.wait()
        term = jnp.dot(h_buf[n], w_buf[n], preferred_element_type=jnp.float32)
        total = term if total is None else total + term
    for part in range(16):
        for sel in range(2):
            at = part * 24 + sel * 12
            o_ref[sel, part * 12 : part * 12 + 12, :] = total[at : at + 12]


def attend_kernel(info_ref, q_ref, cos_ref, sin_ref, *refs):
    mine, near_ref, far_ref, o_ref, buf, s_ref, sems = refs[:4], *refs[4:]
    rows = q_ref.shape[0]
    x, y, core = info_ref[0], info_ref[1], info_ref[2]
    size = near_ref.shape[0]

    def copies(i):
        other = near_ref if i == 0 else far_ref.at[pl.ds((i - 1) * size, size)]
        return [
            pltpu.make_async_copy(mine[i], buf.at[i, core], sems.at[i, 0]),
            pltpu.make_async_copy(other, buf.at[i, 1 - core], sems.at[i, 1]),
        ]

    for i in range(4):

        @pl.when(x >= i)
        def _(i=i):
            for copy in copies(i):
                copy.start()

    sums = q_ref[...]
    q = sums * cos_ref[...] + pltpu.roll(sums, HD // 2, 1) * sin_ref[...]
    q = q.astype(jnp.bfloat16)

    def lanes(v, op):
        out = v[:, :HD]
        for i in range(1, v.shape[1] // HD):
            out = op(out, v[:, i * HD : (i + 1) * HD])
        return out

    def scores(k):
        return lax.dot_general(
            q, k, (((1,), (1,)), ((), ())), preferred_element_type=jnp.float32
        )

    for copy in copies(0):
        copy.wait()
    s = scores(buf[0, 0])
    qp = y * rows + lax.broadcasted_iota(jnp.int32, s.shape, 0)
    kp = lax.broadcasted_iota(jnp.int32, s.shape, 1)
    s = jnp.where(qp >= kp, s, -jnp.inf)
    s_ref[0] = s
    top = lanes(s, jnp.maximum)
    for i in range(1, 4):

        @pl.when(x >= i)
        def _(i=i):
            for copy in copies(i):
                copy.wait()

    def first_pass(i, top):
        s = scores(buf[i, 0])
        s_ref[i] = s
        return jnp.maximum(top, lanes(s, jnp.maximum))

    top = lax.fori_loop(1, x + 1, first_pass, top)
    top = jnp.max(top, axis=1, keepdims=True)
    scale = HD**-0.5 * math.log2(math.e)

    def second_pass(i, state):
        tot, acc = state
        e = jnp.exp2((s_ref[i] - top) * scale)
        return tot + lanes(e, jnp.add), acc + jnp.dot(
            e.astype(jnp.bfloat16), buf[i, 1], preferred_element_type=jnp.float32
        )

    zero = jnp.zeros((rows, HD), jnp.float32)
    tot, acc = lax.fori_loop(0, x + 1, second_pass, (zero, zero))
    o_ref[...] = (acc / jnp.sum(tot, axis=1, keepdims=True)).astype(o_ref.dtype)


def project(info, h, pieces):
    m, depth = h.shape
    hbm = pl.BlockSpec(memory_space=pl.ANY)
    return pl.pallas_call(
        project_kernel,
        in_specs=[pl.BlockSpec(memory_space=pltpu.SMEM)] + [hbm] * 5,
        out_specs=pl.BlockSpec(memory_space=pltpu.VMEM),
        out_shape=jax.ShapeDtypeStruct((2, m // 2, HD), jnp.float32),
        scratch_shapes=[
            pltpu.VMEM((4, m, depth // 4), jnp.bfloat16),
            pltpu.VMEM((4, depth // 4, HD), jnp.bfloat16),
            pltpu.SemaphoreType.DMA((4, 2)),
        ],
        compiler_params=pltpu.CompilerParams(vmem_limit_bytes=48 * 2**20),
        cost_estimate=pl.CostEstimate(
            flops=2 * m * depth * HD, bytes_accessed=2 * depth * (m + HD), transcendentals=0
        ),
        name="project",
    )(info, h, *pieces)


def attend(info, sums, cosine, sine, mine, other):
    vm = pl.BlockSpec(memory_space=pltpu.VMEM)
    return pl.pallas_call(
        attend_kernel,
        in_specs=[pl.BlockSpec(memory_space=pltpu.SMEM), vm, vm, vm]
        + [pl.BlockSpec(memory_space=pl.ANY)] * 6,
        out_specs=vm,
        out_shape=jax.ShapeDtypeStruct(sums.shape, jnp.bfloat16),
        scratch_shapes=[
            pltpu.VMEM((4, 2, 1536, HD), jnp.bfloat16),
            pltpu.VMEM((4, 192, 1536), jnp.float32),
            pltpu.SemaphoreType.DMA((4, 2)),
        ],
        compiler_params=pltpu.CompilerParams(vmem_limit_bytes=40 * 2**20),
        cost_estimate=pl.CostEstimate(
            flops=4 * 192 * 6144 * HD,
            bytes_accessed=4 * 6144 * HD,
            transcendentals=192 * 6144,
        ),
        name="attend",
    )(info, sums, cosine, sine, *mine, *other)


def shift(v, axis, by):
    n = lax.axis_size(axis)
    return lax.ppermute(v, axis, [(i, (i + by) % n) for i in range(n)])


def shift_up(v, axis, by):
    n = lax.axis_size(axis)
    return lax.ppermute(v, axis, [(i, i + by) for i in range(n - by)])


def swap(v, axis):
    return lax.ppermute(v, axis, [(0, 1), (1, 0)])


def body(hidden, query_weight, kv_weight):
    x, yh, yl, z, core = (lax.axis_index(a) for a in AXES)
    y = yh * 4 + yl
    base = (x * 8 + y) * 192
    info = jnp.stack([x, y, core])
    tie = lax.optimization_barrier

    w = lax.all_gather(query_weight, "yl", axis=0, tiled=True)

    hs = hidden.reshape(12, 16, 1024).transpose(1, 0, 2)
    hs, hidden = tie((hs, hidden))
    hs = lax.all_to_all(hs, TP, 0, 0, tiled=True).reshape(192, 1024)

    parts = [hidden[:, i * 2048 : (i + 1) * 2048] for i in range(8)]
    halves = [jnp.concatenate(parts[i::2], axis=1) for i in range(2)]
    keep = jnp.where(yh == 0, halves[0], halves[1])
    come = swap(jnp.where(yh == 0, halves[1], halves[0]), "yh")
    h = jnp.where(
        yh == 0, jnp.concatenate([keep, come], 0), jnp.concatenate([come, keep], 0)
    )
    part = jnp.dot(hs, kv_weight, preferred_element_type=jnp.float32)
    part = part.reshape(8, 24, 2, HD).transpose(0, 2, 1, 3).reshape(16, 24, HD)
    h, w, _ = tie((h, w, part))
    h = lax.all_gather(h, TP, axis=0, tiled=True)

    part = lax.all_to_all(part, TP, 0, 0, tiled=True)
    up, down = shift(w, "x", 1), shift(w, "x", -1)
    rows = jnp.sum(part, axis=0)
    cosine, sine = angles_of(base + z * 24 + jnp.arange(24, dtype=jnp.int32))
    rows = jnp.where(core == 0, rotate(rows, cosine, sine), rows).astype(jnp.bfloat16)
    rows = broadcast_gather(rows, ("yh", "yl", "z")).reshape(1536, HD)
    rows, up, down = tie((rows, up, down))
    cross = [shift(up[:1024], "x", 1), shift(down[1024:], "x", -1)]
    mine = [rows] + [shift_up(rows, "x", d) for d in (1, 2, 3)]

    sums = project(info, h, (w, up, jnp.concatenate(cross, axis=0), down))
    keep = jnp.where(yh == 0, sums[0], sums[1])
    come = swap(jnp.where(yh == 0, sums[1], sums[0]), "yh")
    away, come = tie((mine[1:], come))
    other = [swap(rows, "core"), swap(jnp.concatenate(away, axis=0), "core")]
    cosine, sine = angles_of(base + jnp.arange(192, dtype=jnp.int32))
    cosine = jnp.concatenate([cosine, cosine], axis=1)
    sine = jnp.concatenate([-sine, sine], axis=1)
    return attend(info, keep + come, cosine, sine, mine, other)


def solution(mesh):
    in_specs = (P(AXES, None), P(CTX, TP), P(TP, None))
    out_specs = P(CTX, TP)
    return jax.shard_map(
        body, mesh=fine_mesh(mesh), in_specs=in_specs, out_specs=out_specs, check_vma=False
    )
```

```python
import math

import jax
import jax.numpy as jnp
from jax import lax
from jax.experimental import pallas as pl
from jax.experimental.pallas import tpu as pltpu
from jax.sharding import Mesh
from jax.sharding import PartitionSpec as P

HD = 128
CTX = ("x", "yh", "yl")
TP = ("z", "core")
AXES = CTX + TP


def fine_mesh(mesh):
    return Mesh(mesh.devices.reshape(4, 2, 4, 8, 2), AXES)


def angles_of(positions):
    half = HD // 2
    exponent = jnp.arange(half, dtype=jnp.float32) * (2.0 / HD)
    frequency = jnp.power(jnp.float32(500000.0), -exponent)
    angles = positions.astype(jnp.float32)[:, None] * frequency[None, :]
    return jnp.cos(angles), jnp.sin(angles)


def rotate(field, cosine, sine):
    half = HD // 2
    first, second = field[:, :half], field[:, half:]
    return jnp.concatenate(
        [first * cosine - second * sine, second * cosine + first * sine], axis=1
    )


def broadcast_gather(x, axis):
    n = lax.axis_size(axis)
    return lax.all_to_all(
        jnp.broadcast_to(x[None], (n,) + x.shape), axis, 0, 0, tiled=True
    )


def slabs_kernel(h_ref, o_ref):
    width = o_ref.shape[2]
    for i in range(o_ref.shape[0]):
        o_ref[i] = h_ref[:, i * width : (i + 1) * width]


def halves_kernel(info_ref, h_ref, keep_ref, send_ref):
    yh = info_ref[1] // 4
    for i in range(4):
        low = h_ref[:, i * 4096 : i * 4096 + 2048]
        high = h_ref[:, i * 4096 + 2048 : (i + 1) * 4096]
        keep_ref[:, i * 2048 : (i + 1) * 2048] = jnp.where(yh == 0, low, high)
        send_ref[:, i * 2048 : (i + 1) * 2048] = jnp.where(yh == 0, high, low)


def ends_kernel(up_ref, down_ref, first_ref, last_ref):
    part = first_ref.shape[0]
    first_ref[...] = up_ref[:part]
    last_ref[...] = down_ref[part:]


def small_kernel(kernel, name, outs, args, cost=0):
    vm = pl.BlockSpec(memory_space=pltpu.VMEM)
    smem = pl.BlockSpec(memory_space=pltpu.SMEM)
    return pl.pallas_call(
        kernel,
        in_specs=[smem if a.ndim == 1 else vm for a in args],
        out_specs=[vm] * len(outs),
        out_shape=[jax.ShapeDtypeStruct(o, jnp.bfloat16) for o in outs],
        compiler_params=pltpu.CompilerParams(vmem_limit_bytes=24 * 2**20),
        cost_estimate=pl.CostEstimate(flops=0, bytes_accessed=cost, transcendentals=0),
        name=name,
    )(*args)


def project_kernel(info_ref, h_ref, *refs):
    w_refs, o_ref, h_buf, w_buf, sems = refs[:4], *refs[4:]
    x = info_ref[0]
    copies = []
    for n in range(8):
        at = pl.multiple_of(lax.rem(x + 4 - n // 2, 4) * 2048 + n % 2 * 1024, 1024)
        tile = w_refs[n // 2].at[pl.ds(n % 2 * 1024, 1024)]
        copies.append(
            (
                pltpu.make_async_copy(h_ref.at[:, pl.ds(at, 1024)], h_buf.at[n], sems.at[n, 0]),
                pltpu.make_async_copy(tile, w_buf.at[n], sems.at[n, 1]),
            )
        )
        for copy in copies[n]:
            copy.start()
    total = None
    for n in range(8):
        for copy in copies[n]:
            copy.wait()
        term = jnp.dot(h_buf[n], w_buf[n], preferred_element_type=jnp.float32)
        total = term if total is None else total + term
    for part in range(16):
        for sel in range(2):
            at = part * 24 + sel * 12
            o_ref[sel, part * 12 : part * 12 + 12, :] = total[at : at + 12]


def attend_kernel(info_ref, q_ref, cos_ref, sin_ref, *refs):
    mine, other_ref, o_ref, buf, s_ref, sems = refs[:4], *refs[4:]
    rows = q_ref.shape[0]
    x, y, core = info_ref[0], info_ref[1], info_ref[2]
    size = mine[0].shape[0]

    def copies(i):
        other = other_ref.at[pl.ds(i * size, size)]
        return [
            pltpu.make_async_copy(mine[i], buf.at[i, core], sems.at[i, 0]),
            pltpu.make_async_copy(other, buf.at[i, 1 - core], sems.at[i, 1]),
        ]

    for i in range(4):

        @pl.when(x >= i)
        def _(i=i):
            for copy in copies(i):
                copy.start()

    sums = q_ref[...]
    q = sums * cos_ref[...] + pltpu.roll(sums, HD // 2, 1) * sin_ref[...]
    q = q.astype(jnp.bfloat16)

    def lanes(v, op):
        out = v[:, :HD]
        for i in range(1, v.shape[1] // HD):
            out = op(out, v[:, i * HD : (i + 1) * HD])
        return out

    def scores(k):
        return lax.dot_general(
            q, k, (((1,), (1,)), ((), ())), preferred_element_type=jnp.float32
        )

    for copy in copies(0):
        copy.wait()
    s = scores(buf[0, 0])
    qp = y * rows + lax.broadcasted_iota(jnp.int32, s.shape, 0)
    kp = lax.broadcasted_iota(jnp.int32, s.shape, 1)
    s = jnp.where(qp >= kp, s, -jnp.inf)
    s_ref[0] = s
    top = lanes(s, jnp.maximum)
    for i in range(1, 4):

        @pl.when(x >= i)
        def _(i=i):
            for copy in copies(i):
                copy.wait()

    def first_pass(i, top):
        s = scores(buf[i, 0])
        s_ref[i] = s
        return jnp.maximum(top, lanes(s, jnp.maximum))

    top = lax.fori_loop(1, x + 1, first_pass, top)
    top = jnp.max(top, axis=1, keepdims=True)
    scale = HD**-0.5 * math.log2(math.e)

    def second_pass(i, state):
        tot, acc = state
        e = jnp.exp2((s_ref[i] - top) * scale)
        return tot + lanes(e, jnp.add), acc + jnp.dot(
            e.astype(jnp.bfloat16), buf[i, 1], preferred_element_type=jnp.float32
        )

    zero = jnp.zeros((rows, HD), jnp.float32)
    tot, acc = lax.fori_loop(0, x + 1, second_pass, (zero, zero))
    o_ref[...] = (acc / jnp.sum(tot, axis=1, keepdims=True)).astype(o_ref.dtype)


def project(info, h, pieces):
    m, depth = h.shape
    hbm = pl.BlockSpec(memory_space=pl.ANY)
    return pl.pallas_call(
        project_kernel,
        in_specs=[pl.BlockSpec(memory_space=pltpu.SMEM)] + [hbm] * 5,
        out_specs=pl.BlockSpec(memory_space=pltpu.VMEM),
        out_shape=jax.ShapeDtypeStruct((2, m // 2, HD), jnp.float32),
        scratch_shapes=[
            pltpu.VMEM((8, m, depth // 8), jnp.bfloat16),
            pltpu.VMEM((8, depth // 8, HD), jnp.bfloat16),
            pltpu.SemaphoreType.DMA((8, 2)),
        ],
        compiler_params=pltpu.CompilerParams(vmem_limit_bytes=48 * 2**20),
        cost_estimate=pl.CostEstimate(
            flops=2 * m * depth * HD, bytes_accessed=2 * depth * (m + HD), transcendentals=0
        ),
        name="project",
    )(info, h, *pieces)


def attend(info, sums, cosine, sine, mine, other):
    vm = pl.BlockSpec(memory_space=pltpu.VMEM)
    return pl.pallas_call(
        attend_kernel,
        in_specs=[pl.BlockSpec(memory_space=pltpu.SMEM), vm, vm, vm]
        + [pl.BlockSpec(memory_space=pl.ANY)] * 5,
        out_specs=vm,
        out_shape=jax.ShapeDtypeStruct(sums.shape, jnp.bfloat16),
        scratch_shapes=[
            pltpu.VMEM((4, 2, 1536, HD), jnp.bfloat16),
            pltpu.VMEM((4, 192, 1536), jnp.float32),
            pltpu.SemaphoreType.DMA((4, 2)),
        ],
        compiler_params=pltpu.CompilerParams(vmem_limit_bytes=40 * 2**20),
        cost_estimate=pl.CostEstimate(
            flops=4 * 192 * 6144 * HD,
            bytes_accessed=4 * 6144 * HD,
            transcendentals=192 * 6144,
        ),
        name="attend",
    )(info, sums, cosine, sine, *mine, other)


def shift(v, axis, by):
    n = lax.axis_size(axis)
    return lax.ppermute(v, axis, [(i, (i + by) % n) for i in range(n)])


def shift_up(v, axis, by):
    n = lax.axis_size(axis)
    return lax.ppermute(v, axis, [(i, i + by) for i in range(n - by)])


def swap(v, axis):
    return lax.ppermute(v, axis, [(0, 1), (1, 0)])


def body(hidden, query_weight, kv_weight):
    x, yh, yl, z, core = (lax.axis_index(a) for a in AXES)
    y = yh * 4 + yl
    base = (x * 8 + y) * 192
    info = jnp.stack([x, y, core])
    tie = lax.optimization_barrier

    w = lax.all_gather(query_weight, "yl", axis=0, tiled=True)

    (hs,) = small_kernel(slabs_kernel, "slabs", [(16, 12, 1024)], (hidden,), 2**20)
    hs = lax.all_to_all(hs, TP, 0, 0, tiled=True).reshape(192, 1024)

    keep, send = small_kernel(
        halves_kernel, "halves", [(12, 8192)] * 2, (info, hidden), 100 * 2**20
    )
    come = swap(send, "yh")
    h = jnp.where(
        yh == 0, jnp.concatenate([keep, come], 0), jnp.concatenate([come, keep], 0)
    )
    part = jnp.dot(hs, kv_weight, preferred_element_type=jnp.float32)
    part = part.reshape(8, 24, 2, HD).transpose(0, 2, 1, 3).reshape(16, 24, HD)
    h, w, _ = tie((h, w, part))
    h = lax.all_gather(h, TP, axis=0, tiled=True)

    part = lax.all_to_all(part, TP, 0, 0, tiled=True)
    up, down = shift(w, "x", 1), shift(w, "x", -1)
    rows = jnp.sum(part, axis=0)
    cosine, sine = angles_of(base + z * 24 + jnp.arange(24, dtype=jnp.int32))
    rows = jnp.where(core == 0, rotate(rows, cosine, sine), rows).astype(jnp.bfloat16)
    rows = broadcast_gather(rows, ("yh", "yl", "z")).reshape(1536, HD)
    first, last = small_kernel(
        ends_kernel, "ends", [(1024, HD)] * 2, (up, down), 60 * 2**20
    )
    cross = [shift(first, "x", 1), shift(last, "x", -1)]
    rows, cross = tie((rows, cross))
    mine = [rows] + [shift_up(rows, "x", d) for d in (1, 2, 3)]

    sums = project(info, h, (w, up, jnp.concatenate(cross, axis=0), down))
    keep = jnp.where(yh == 0, sums[0], sums[1])
    come = swap(jnp.where(yh == 0, sums[1], sums[0]), "yh")
    away, come = tie((mine[1:], come))
    other = swap(jnp.concatenate([rows] + away, axis=0), "core")
    cosine, sine = angles_of(base + jnp.arange(192, dtype=jnp.int32))
    cosine = jnp.concatenate([cosine, cosine], axis=1)
    sine = jnp.concatenate([-sine, sine], axis=1)
    return attend(info, keep + come, cosine, sine, mine, other)


def solution(mesh):
    in_specs = (P(AXES, None), P(CTX, TP), P(TP, None))
    out_specs = P(CTX, TP)
    return jax.shard_map(
        body, mesh=fine_mesh(mesh), in_specs=in_specs, out_specs=out_specs, check_vma=False
    )
```

```python
import math

import jax
import jax.numpy as jnp
from jax import lax
from jax.experimental import pallas as pl
from jax.experimental.pallas import tpu as pltpu
from jax.sharding import Mesh
from jax.sharding import PartitionSpec as P

HD = 128
CTX = ("x", "yq", "yp")
TP = ("z", "core")
PAIR = ("yp", "z", "core")
AXES = CTX + TP


def fine_mesh(mesh):
    return Mesh(mesh.devices.reshape(4, 4, 2, 8, 2), AXES)


def angles_of(positions):
    half = HD // 2
    exponent = jnp.arange(half, dtype=jnp.float32) * (2.0 / HD)
    frequency = jnp.power(jnp.float32(500000.0), -exponent)
    angles = positions.astype(jnp.float32)[:, None] * frequency[None, :]
    return jnp.cos(angles), jnp.sin(angles)


def rotate(field, cosine, sine):
    half = HD // 2
    first, second = field[:, :half], field[:, half:]
    return jnp.concatenate(
        [first * cosine - second * sine, second * cosine + first * sine], axis=1
    )


def broadcast_gather(x, axis):
    n = lax.axis_size(axis)
    return lax.all_to_all(
        jnp.broadcast_to(x[None], (n,) + x.shape), axis, 0, 0, tiled=True
    )


def slabs_kernel(h_ref, o_ref):
    for yp in range(2):
        for t in range(16):
            at = (2 * t + yp) * 512
            o_ref[yp * 16 + t] = h_ref[:, at : at + 512]


def mix_kernel(info_ref, x_ref, w_ref, rows_ref, o_ref, buf):
    yp = lax.rem(info_ref[1], 2)
    for i in range(32):
        buf[i * 12 : (i + 1) * 12, :] = x_ref[i].astype(jnp.float32)
    rows = buf[...].astype(jnp.bfloat16)
    rows_ref[...] = rows
    w = w_ref[pl.ds(pl.multiple_of(yp * 512, 512), 512), :]
    sums = jnp.dot(rows, w, preferred_element_type=jnp.float32)
    for i in range(16):
        for k in range(2):
            o_ref[2 * i + k] = sums[i * 24 : (i + 1) * 24, k * HD : (k + 1) * HD]


def mix(info, x, w):
    vm = pl.BlockSpec(memory_space=pltpu.VMEM)
    return pl.pallas_call(
        mix_kernel,
        in_specs=[pl.BlockSpec(memory_space=pltpu.SMEM), vm, vm],
        out_specs=[vm, vm],
        out_shape=[
            jax.ShapeDtypeStruct((384, 512), jnp.bfloat16),
            jax.ShapeDtypeStruct((32, 24, HD), jnp.float32),
        ],
        scratch_shapes=[pltpu.VMEM((384, 512), jnp.float32)],
        compiler_params=pltpu.CompilerParams(vmem_limit_bytes=24 * 2**20),
        cost_estimate=pl.CostEstimate(
            flops=2 * 384 * 512 * 256, bytes_accessed=2**20, transcendentals=0
        ),
        name="mix",
    )(info, x, w)


def ends_kernel(up_ref, down_ref, first_ref, last_ref):
    part = first_ref.shape[0]
    first_ref[...] = up_ref[:part]
    last_ref[...] = down_ref[part:]


def join_kernel(*refs):
    size = refs[0].shape[0]
    for i, ref in enumerate(refs[:-1]):
        refs[-1][i * size : (i + 1) * size] = ref[...]


def small_kernel(kernel, name, outs, args):
    vm = pl.BlockSpec(memory_space=pltpu.VMEM)
    smem = pl.BlockSpec(memory_space=pltpu.SMEM)
    return pl.pallas_call(
        kernel,
        in_specs=[smem if a.ndim == 1 else vm for a in args],
        out_specs=[vm] * len(outs),
        out_shape=[jax.ShapeDtypeStruct(o, jnp.bfloat16) for o in outs],
        compiler_params=pltpu.CompilerParams(vmem_limit_bytes=24 * 2**20),
        cost_estimate=pl.CostEstimate(flops=0, bytes_accessed=2**20, transcendentals=0),
        name=name,
    )(*args)


def project_kernel(info_ref, h_ref, *refs):
    w_refs, o_ref, h_buf, w_buf, sems = refs[:4], *refs[4:]
    x = info_ref[0]
    copies = []
    for n in range(4):
        at = lax.rem(x + 4 - n, 4) * 4
        copies.append(
            (
                pltpu.make_async_copy(h_ref.at[pl.ds(at, 4)], h_buf.at[n], sems.at[n, 0]),
                pltpu.make_async_copy(w_refs[n], w_buf.at[n], sems.at[n, 1]),
            )
        )
        for copy in copies[n]:
            copy.start()
    total = None
    for n in range(4):
        for copy in copies[n]:
            copy.wait()
        a = jnp.concatenate([h_buf[n, i] for i in range(4)], axis=1)
        term = jnp.dot(a, w_buf[n], preferred_element_type=jnp.float32)
        total = term if total is None else total + term
    for sel in range(2):
        o_ref[sel] = total[sel * 192 : (sel + 1) * 192]


def attend_kernel(info_ref, q_ref, cos_ref, sin_ref, *refs):
    mine, other_ref, o_ref, buf, s_ref, sems = refs[:4], *refs[4:]
    rows = q_ref.shape[0]
    x, y, core = info_ref[0], info_ref[1], info_ref[2]
    size = mine[0].shape[0]

    def copies(i):
        other = other_ref.at[pl.ds(i * size, size)]
        return [
            pltpu.make_async_copy(mine[i], buf.at[i, core], sems.at[i, 0]),
            pltpu.make_async_copy(other, buf.at[i, 1 - core], sems.at[i, 1]),
        ]

    for i in range(4):

        @pl.when(x >= i)
        def _(i=i):
            for copy in copies(i):
                copy.start()

    sums = q_ref[...]
    q = sums * cos_ref[...] + pltpu.roll(sums, HD // 2, 1) * sin_ref[...]
    q = q.astype(jnp.bfloat16)

    def lanes(v, op):
        out = v[:, :HD]
        for i in range(1, v.shape[1] // HD):
            out = op(out, v[:, i * HD : (i + 1) * HD])
        return out

    def scores(k):
        return lax.dot_general(
            q, k, (((1,), (1,)), ((), ())), preferred_element_type=jnp.float32
        )

    for copy in copies(0):
        copy.wait()
    s = scores(buf[0, 0])
    qp = y * rows + lax.broadcasted_iota(jnp.int32, s.shape, 0)
    kp = lax.broadcasted_iota(jnp.int32, s.shape, 1)
    s = jnp.where(qp >= kp, s, -jnp.inf)
    s_ref[0] = s
    top = lanes(s, jnp.maximum)
    for i in range(1, 4):

        @pl.when(x >= i)
        def _(i=i):
            for copy in copies(i):
                copy.wait()

    def first_pass(i, top):
        s = scores(buf[i, 0])
        s_ref[i] = s
        return jnp.maximum(top, lanes(s, jnp.maximum))

    top = lax.fori_loop(1, x + 1, first_pass, top)
    top = jnp.max(top, axis=1, keepdims=True)
    scale = HD**-0.5 * math.log2(math.e)

    def second_pass(i, state):
        tot, acc = state
        e = jnp.exp2((s_ref[i] - top) * scale)
        return tot + lanes(e, jnp.add), acc + jnp.dot(
            e.astype(jnp.bfloat16), buf[i, 1], preferred_element_type=jnp.float32
        )

    zero = jnp.zeros((rows, HD), jnp.float32)
    tot, acc = lax.fori_loop(0, x + 1, second_pass, (zero, zero))
    o_ref[...] = (acc / jnp.sum(tot, axis=1, keepdims=True)).astype(o_ref.dtype)


def project(info, h, pieces):
    count, m, part = h.shape
    hbm = pl.BlockSpec(memory_space=pl.ANY)
    return pl.pallas_call(
        project_kernel,
        in_specs=[pl.BlockSpec(memory_space=pltpu.SMEM)] + [hbm] * 5,
        out_specs=pl.BlockSpec(memory_space=pltpu.VMEM),
        out_shape=jax.ShapeDtypeStruct((2, m // 2, HD), jnp.float32),
        scratch_shapes=[
            pltpu.VMEM((4, count // 4, m, part), jnp.bfloat16),
            pltpu.VMEM((4, count // 4 * part, HD), jnp.bfloat16),
            pltpu.SemaphoreType.DMA((4, 2)),
        ],
        compiler_params=pltpu.CompilerParams(vmem_limit_bytes=48 * 2**20),
        cost_estimate=pl.CostEstimate(
            flops=2 * m * count * part * HD,
            bytes_accessed=2 * count * part * (m + HD),
            transcendentals=0,
        ),
        name="project",
    )(info, h, *pieces)


def attend(info, sums, cosine, sine, mine, other):
    vm = pl.BlockSpec(memory_space=pltpu.VMEM)
    return pl.pallas_call(
        attend_kernel,
        in_specs=[pl.BlockSpec(memory_space=pltpu.SMEM), vm, vm, vm]
        + [pl.BlockSpec(memory_space=pl.ANY)] * 5,
        out_specs=vm,
        out_shape=jax.ShapeDtypeStruct(sums.shape, jnp.bfloat16),
        scratch_shapes=[
            pltpu.VMEM((4, 2, 1536, HD), jnp.bfloat16),
            pltpu.VMEM((4, 192, 1536), jnp.float32),
            pltpu.SemaphoreType.DMA((4, 2)),
        ],
        compiler_params=pltpu.CompilerParams(vmem_limit_bytes=40 * 2**20),
        cost_estimate=pl.CostEstimate(
            flops=4 * 192 * 6144 * HD,
            bytes_accessed=4 * 6144 * HD,
            transcendentals=192 * 6144,
        ),
        name="attend",
    )(info, sums, cosine, sine, *mine, other)


def shift(v, axis, by):
    n = lax.axis_size(axis)
    return lax.ppermute(v, axis, [(i, (i + by) % n) for i in range(n)])


def shift_up(v, axis, by):
    n = lax.axis_size(axis)
    return lax.ppermute(v, axis, [(i, i + by) for i in range(n - by)])


def swap(v, axis):
    return lax.ppermute(v, axis, [(0, 1), (1, 0)])


def body(hidden, query_weight, kv_weight):
    x, yq, yp, z, core = (lax.axis_index(a) for a in AXES)
    y = yq * 2 + yp
    base = (x * 8 + y) * 192
    info = jnp.stack([x, y, core])
    tie = lax.optimization_barrier

    w = lax.all_gather(query_weight, "yq", axis=0, tiled=True)

    (hs,) = small_kernel(slabs_kernel, "slabs", [(32, 12, 512)], (hidden,))
    hs = lax.all_to_all(hs, PAIR, 0, 0, tiled=True)
    h, part = mix(info, hs, kv_weight)
    h, w, part = tie((h, w, part))
    h = lax.all_gather(h, TP, axis=0, tiled=False)

    part = lax.all_to_all(part, PAIR, 0, 0, tiled=True)
    up, down = shift(w, "x", 1), shift(w, "x", -1)
    rows = jnp.sum(part, axis=0)
    cosine, sine = angles_of(base + z * 24 + jnp.arange(24, dtype=jnp.int32))
    rows = jnp.where(core == 0, rotate(rows, cosine, sine), rows).astype(jnp.bfloat16)
    rows = broadcast_gather(rows, ("yq", "yp", "z")).reshape(1536, HD)
    first, last = small_kernel(ends_kernel, "ends", [(1024, HD)] * 2, (up, down))
    cross = [shift(first, "x", 1), shift(last, "x", -1)]
    rows, cross = tie((rows, cross))
    mine = [rows] + [shift_up(rows, "x", d) for d in (1, 2, 3)]

    sums = project(info, h, (w, up, jnp.concatenate(cross, axis=0), down))
    keep = jnp.where(yp == 0, sums[0], sums[1])
    come = swap(jnp.where(yp == 0, sums[1], sums[0]), "yp")
    away, come = tie((mine[1:], come))
    (other,) = small_kernel(join_kernel, "join", [(6144, HD)], (rows, *away))
    other = swap(other, "core")
    cosine, sine = angles_of(base + jnp.arange(192, dtype=jnp.int32))
    cosine = jnp.concatenate([cosine, cosine], axis=1)
    sine = jnp.concatenate([-sine, sine], axis=1)
    return attend(info, keep + come, cosine, sine, mine, other)


def solution(mesh):
    in_specs = (P(AXES, None), P(CTX, TP), P(TP, None))
    out_specs = P(CTX, TP)
    return jax.shard_map(
        body, mesh=fine_mesh(mesh), in_specs=in_specs, out_specs=out_specs, check_vma=False
    )
```

```python
import math

import jax
import jax.numpy as jnp
from jax import lax
from jax.experimental import pallas as pl
from jax.experimental.pallas import tpu as pltpu
from jax.sharding import Mesh
from jax.sharding import PartitionSpec as P

HD = 128
CTX = ("x", "yq", "yp")
TP = ("z", "core")
PAIR = ("yp", "z", "core")
AXES = CTX + TP


def fine_mesh(mesh):
    return Mesh(mesh.devices.reshape(4, 4, 2, 8, 2), AXES)


def angles_of(positions):
    half = HD // 2
    exponent = jnp.arange(half, dtype=jnp.float32) * (2.0 / HD)
    frequency = jnp.power(jnp.float32(500000.0), -exponent)
    angles = positions.astype(jnp.float32)[:, None] * frequency[None, :]
    return jnp.cos(angles), jnp.sin(angles)


def rotate(field, cosine, sine):
    half = HD // 2
    first, second = field[:, :half], field[:, half:]
    return jnp.concatenate(
        [first * cosine - second * sine, second * cosine + first * sine], axis=1
    )


def broadcast_gather(x, axis):
    n = lax.axis_size(axis)
    return lax.all_to_all(
        jnp.broadcast_to(x[None], (n,) + x.shape), axis, 0, 0, tiled=True
    )


def slabs_kernel(h_ref, o_ref):
    for yp in range(2):
        for t in range(16):
            at = (2 * t + yp) * 512
            o_ref[yp * 16 + t] = h_ref[:, at : at + 512]


def mix_kernel(info_ref, x_ref, w_ref, rows_ref, o_ref, buf):
    yp = lax.rem(info_ref[1], 2)
    for i in range(32):
        buf[i * 12 : (i + 1) * 12, :] = x_ref[i].astype(jnp.float32)
    rows = buf[...].astype(jnp.bfloat16)
    rows_ref[...] = rows
    w = w_ref[pl.ds(pl.multiple_of(yp * 512, 512), 512), :]
    sums = jnp.dot(rows, w, preferred_element_type=jnp.float32)
    for i in range(16):
        for k in range(2):
            o_ref[2 * i + k] = sums[i * 24 : (i + 1) * 24, k * HD : (k + 1) * HD]


def mix(info, x, w):
    vm = pl.BlockSpec(memory_space=pltpu.VMEM)
    return pl.pallas_call(
        mix_kernel,
        in_specs=[pl.BlockSpec(memory_space=pltpu.SMEM), vm, vm],
        out_specs=[vm, vm],
        out_shape=[
            jax.ShapeDtypeStruct((384, 512), jnp.bfloat16),
            jax.ShapeDtypeStruct((32, 24, HD), jnp.float32),
        ],
        scratch_shapes=[pltpu.VMEM((384, 512), jnp.float32)],
        compiler_params=pltpu.CompilerParams(vmem_limit_bytes=24 * 2**20),
        cost_estimate=pl.CostEstimate(
            flops=2 * 384 * 512 * 256, bytes_accessed=2**20, transcendentals=0
        ),
        name="mix",
    )(info, x, w)


def ends_kernel(up_ref, down_ref, first_ref, last_ref):
    part = first_ref.shape[0]
    first_ref[...] = up_ref[:part]
    last_ref[...] = down_ref[part:]


def join_kernel(*refs):
    size = refs[0].shape[0]
    for i, ref in enumerate(refs[:-1]):
        refs[-1][i * size : (i + 1) * size] = ref[...]


def small_kernel(kernel, name, outs, args):
    vm = pl.BlockSpec(memory_space=pltpu.VMEM)
    smem = pl.BlockSpec(memory_space=pltpu.SMEM)
    return pl.pallas_call(
        kernel,
        in_specs=[smem if a.ndim == 1 else vm for a in args],
        out_specs=[vm] * len(outs),
        out_shape=[jax.ShapeDtypeStruct(o, jnp.bfloat16) for o in outs],
        compiler_params=pltpu.CompilerParams(vmem_limit_bytes=24 * 2**20),
        cost_estimate=pl.CostEstimate(flops=0, bytes_accessed=2**20, transcendentals=0),
        name=name,
    )(*args)


def project_kernel(info_ref, h_ref, *refs):
    w_refs, o_ref, buf, sems = refs[:4], *refs[4:]
    x, yq = info_ref[0], info_ref[1] // 2
    copies = []
    for n in range(4):
        for back in range(4):
            block = lax.rem(x + 4 - n, 4) * 4 + lax.rem(yq + 4 - back, 4)
            i = 4 * n + back
            copies.append(pltpu.make_async_copy(h_ref.at[block], buf.at[i], sems.at[i]))
            copies[-1].start()
    total = None
    for n in range(4):
        for half in range(2):
            for i in range(2):
                copies[4 * n + 2 * half + i].wait()
            a = jnp.concatenate([buf[4 * n + 2 * half + i] for i in range(2)], axis=1)
            w = w_refs[n][half * 1024 : (half + 1) * 1024]
            term = jnp.dot(a, w, preferred_element_type=jnp.float32)
            total = term if total is None else total + term
    for sel in range(2):
        o_ref[sel] = total[sel * 192 : (sel + 1) * 192]


def attend_kernel(info_ref, q_ref, cos_ref, sin_ref, *refs):
    mine, other_ref, o_ref, buf, s_ref, sems = refs[:4], *refs[4:]
    rows = q_ref.shape[0]
    x, y, core = info_ref[0], info_ref[1], info_ref[2]
    size = mine[0].shape[0]

    def copies(i):
        other = other_ref.at[pl.ds(i * size, size)]
        return [
            pltpu.make_async_copy(mine[i], buf.at[i, core], sems.at[i, 0]),
            pltpu.make_async_copy(other, buf.at[i, 1 - core], sems.at[i, 1]),
        ]

    for i in range(4):

        @pl.when(x >= i)
        def _(i=i):
            for copy in copies(i):
                copy.start()

    sums = q_ref[...]
    q = sums * cos_ref[...] + pltpu.roll(sums, HD // 2, 1) * sin_ref[...]
    q = q.astype(jnp.bfloat16)

    def lanes(v, op):
        out = v[:, :HD]
        for i in range(1, v.shape[1] // HD):
            out = op(out, v[:, i * HD : (i + 1) * HD])
        return out

    def scores(k):
        return lax.dot_general(
            q, k, (((1,), (1,)), ((), ())), preferred_element_type=jnp.float32
        )

    for copy in copies(0):
        copy.wait()
    s = scores(buf[0, 0])
    qp = y * rows + lax.broadcasted_iota(jnp.int32, s.shape, 0)
    kp = lax.broadcasted_iota(jnp.int32, s.shape, 1)
    s = jnp.where(qp >= kp, s, -jnp.inf)
    s_ref[0] = s
    top = lanes(s, jnp.maximum)
    for i in range(1, 4):

        @pl.when(x >= i)
        def _(i=i):
            for copy in copies(i):
                copy.wait()

    def first_pass(i, top):
        s = scores(buf[i, 0])
        s_ref[i] = s
        return jnp.maximum(top, lanes(s, jnp.maximum))

    top = lax.fori_loop(1, x + 1, first_pass, top)
    top = jnp.max(top, axis=1, keepdims=True)
    scale = HD**-0.5 * math.log2(math.e)

    def second_pass(i, state):
        tot, acc = state
        e = jnp.exp2((s_ref[i] - top) * scale)
        return tot + lanes(e, jnp.add), acc + jnp.dot(
            e.astype(jnp.bfloat16), buf[i, 1], preferred_element_type=jnp.float32
        )

    zero = jnp.zeros((rows, HD), jnp.float32)
    tot, acc = lax.fori_loop(0, x + 1, second_pass, (zero, zero))
    o_ref[...] = (acc / jnp.sum(tot, axis=1, keepdims=True)).astype(o_ref.dtype)


def project(info, h, pieces):
    count, m, part = h.shape
    vm = pl.BlockSpec(memory_space=pltpu.VMEM)
    return pl.pallas_call(
        project_kernel,
        in_specs=[
            pl.BlockSpec(memory_space=pltpu.SMEM),
            pl.BlockSpec(memory_space=pl.ANY),
        ]
        + [vm] * 4,
        out_specs=vm,
        out_shape=jax.ShapeDtypeStruct((2, m // 2, HD), jnp.float32),
        scratch_shapes=[
            pltpu.VMEM(h.shape, jnp.bfloat16),
            pltpu.SemaphoreType.DMA((count,)),
        ],
        compiler_params=pltpu.CompilerParams(vmem_limit_bytes=32 * 2**20),
        cost_estimate=pl.CostEstimate(
            flops=2 * m * count * part * HD,
            bytes_accessed=2 * count * part * (m + HD),
            transcendentals=0,
        ),
        name="project",
    )(info, h, *pieces)


def attend(info, sums, cosine, sine, mine, other):
    vm = pl.BlockSpec(memory_space=pltpu.VMEM)
    return pl.pallas_call(
        attend_kernel,
        in_specs=[pl.BlockSpec(memory_space=pltpu.SMEM), vm, vm, vm]
        + [pl.BlockSpec(memory_space=pl.ANY)] * 5,
        out_specs=vm,
        out_shape=jax.ShapeDtypeStruct(sums.shape, jnp.bfloat16),
        scratch_shapes=[
            pltpu.VMEM((4, 2, 1536, HD), jnp.bfloat16),
            pltpu.VMEM((4, 192, 1536), jnp.float32),
            pltpu.SemaphoreType.DMA((4, 2)),
        ],
        compiler_params=pltpu.CompilerParams(vmem_limit_bytes=40 * 2**20),
        cost_estimate=pl.CostEstimate(
            flops=4 * 192 * 6144 * HD,
            bytes_accessed=4 * 6144 * HD,
            transcendentals=192 * 6144,
        ),
        name="attend",
    )(info, sums, cosine, sine, *mine, other)


def shift(v, axis, by):
    n = lax.axis_size(axis)
    return lax.ppermute(v, axis, [(i, (i + by) % n) for i in range(n)])


def shift_up(v, axis, by):
    n = lax.axis_size(axis)
    return lax.ppermute(v, axis, [(i, i + by) for i in range(n - by)])


def swap(v, axis):
    return lax.ppermute(v, axis, [(0, 1), (1, 0)])


def body(hidden, query_weight, kv_weight):
    x, yq, yp, z, core = (lax.axis_index(a) for a in AXES)
    y = yq * 2 + yp
    base = (x * 8 + y) * 192
    info = jnp.stack([x, y, core])
    tie = lax.optimization_barrier

    (hs,) = small_kernel(slabs_kernel, "slabs", [(32, 12, 512)], (hidden,))
    hs, w = tie((hs, query_weight))
    hs = lax.all_to_all(hs, PAIR, 0, 0, tiled=True)

    w = jnp.concatenate([w] + [shift(w, "yq", d) for d in (1, 2, 3)], axis=0)
    h, part = mix(info, hs, kv_weight)
    w, part = tie((w, part))
    h = lax.all_gather(h, TP, axis=0, tiled=False)

    part = lax.all_to_all(part, PAIR, 0, 0, tiled=True)
    up, down = shift(w, "x", 1), shift(w, "x", -1)
    rows = jnp.sum(part, axis=0)
    cosine, sine = angles_of(base + z * 24 + jnp.arange(24, dtype=jnp.int32))
    rows = jnp.where(core == 0, rotate(rows, cosine, sine), rows).astype(jnp.bfloat16)
    rows = broadcast_gather(rows, ("yq", "yp", "z")).reshape(1536, HD)
    first, last = small_kernel(ends_kernel, "ends", [(1024, HD)] * 2, (up, down))
    cross = [shift(first, "x", 1), shift(last, "x", -1)]
    rows, cross = tie((rows, cross))
    mine = [rows] + [shift_up(rows, "x", d) for d in (1, 2, 3)]

    sums = project(info, h, (w, up, jnp.concatenate(cross, axis=0), down))
    keep = jnp.where(yp == 0, sums[0], sums[1])
    come = swap(jnp.where(yp == 0, sums[1], sums[0]), "yp")
    away, sums = tie((mine[1:], sums))
    (other,) = small_kernel(join_kernel, "join", [(6144, HD)], (rows, *away))
    other = swap(other, "core")
    cosine, sine = angles_of(base + jnp.arange(192, dtype=jnp.int32))
    cosine = jnp.concatenate([cosine, cosine], axis=1)
    sine = jnp.concatenate([-sine, sine], axis=1)
    return attend(info, keep + come, cosine, sine, mine, other)


def solution(mesh):
    in_specs = (P(AXES, None), P(CTX, TP), P(TP, None))
    out_specs = P(CTX, TP)
    return jax.shard_map(
        body, mesh=fine_mesh(mesh), in_specs=in_specs, out_specs=out_specs, check_vma=False
    )
```

```python
import math

import jax
import jax.numpy as jnp
from jax import lax
from jax.experimental import pallas as pl
from jax.experimental.pallas import tpu as pltpu
from jax.sharding import Mesh
from jax.sharding import PartitionSpec as P

HD = 128
CTX = ("x", "yq", "yp")
TP = ("z", "core")
PAIR = ("yp", "z", "core")
AXES = CTX + TP


def fine_mesh(mesh):
    return Mesh(mesh.devices.reshape(4, 4, 2, 8, 2), AXES)


def angles_of(positions):
    half = HD // 2
    exponent = jnp.arange(half, dtype=jnp.float32) * (2.0 / HD)
    frequency = jnp.power(jnp.float32(500000.0), -exponent)
    angles = positions.astype(jnp.float32)[:, None] * frequency[None, :]
    return jnp.cos(angles), jnp.sin(angles)


def rotate(field, cosine, sine):
    half = HD // 2
    first, second = field[:, :half], field[:, half:]
    return jnp.concatenate(
        [first * cosine - second * sine, second * cosine + first * sine], axis=1
    )


def broadcast_gather(x, axis):
    n = lax.axis_size(axis)
    return lax.all_to_all(
        jnp.broadcast_to(x[None], (n,) + x.shape), axis, 0, 0, tiled=True
    )


def slabs_kernel(h_ref, o_ref):
    for yp in range(2):
        for t in range(16):
            at = (2 * t + yp) * 512
            o_ref[yp * 16 + t] = h_ref[:, at : at + 512]


def mix_kernel(info_ref, x_ref, w_ref, rows_ref, o_ref, buf):
    yp = lax.rem(info_ref[1], 2)
    for i in range(32):
        buf[i * 12 : (i + 1) * 12, :] = x_ref[i].astype(jnp.float32)
    rows = buf[...].astype(jnp.bfloat16)
    rows_ref[...] = rows
    w = w_ref[pl.ds(pl.multiple_of(yp * 512, 512), 512), :]
    sums = jnp.dot(rows, w, preferred_element_type=jnp.float32)
    for i in range(16):
        for k in range(2):
            o_ref[2 * i + k] = sums[i * 24 : (i + 1) * 24, k * HD : (k + 1) * HD]


def mix(info, x, w):
    vm = pl.BlockSpec(memory_space=pltpu.VMEM)
    return pl.pallas_call(
        mix_kernel,
        in_specs=[pl.BlockSpec(memory_space=pltpu.SMEM), vm, vm],
        out_specs=[vm, vm],
        out_shape=[
            jax.ShapeDtypeStruct((384, 512), jnp.bfloat16),
            jax.ShapeDtypeStruct((32, 24, HD), jnp.float32),
        ],
        scratch_shapes=[pltpu.VMEM((384, 512), jnp.float32)],
        compiler_params=pltpu.CompilerParams(vmem_limit_bytes=24 * 2**20),
        cost_estimate=pl.CostEstimate(
            flops=2 * 384 * 512 * 256, bytes_accessed=2**20, transcendentals=0
        ),
        name="mix",
    )(info, x, w)


def ends_kernel(up_ref, down_ref, first_ref, last_ref):
    part = first_ref.shape[0]
    first_ref[...] = up_ref[:part]
    last_ref[...] = down_ref[part:]


def join_kernel(*refs):
    size = refs[0].shape[0]
    for i, ref in enumerate(refs[:-1]):
        refs[-1][i * size : (i + 1) * size] = ref[...]


def small_kernel(kernel, name, outs, args):
    vm = pl.BlockSpec(memory_space=pltpu.VMEM)
    smem = pl.BlockSpec(memory_space=pltpu.SMEM)
    return pl.pallas_call(
        kernel,
        in_specs=[smem if a.ndim == 1 else vm for a in args],
        out_specs=[vm] * len(outs),
        out_shape=[jax.ShapeDtypeStruct(o, jnp.bfloat16) for o in outs],
        compiler_params=pltpu.CompilerParams(vmem_limit_bytes=24 * 2**20),
        cost_estimate=pl.CostEstimate(flops=0, bytes_accessed=2**20, transcendentals=0),
        name=name,
    )(*args)


def project_kernel(info_ref, h_ref, *refs):
    w_refs, o_ref, h_buf, w_buf, sems = refs[:4], *refs[4:]
    x = info_ref[0]
    copies = []
    for n in range(4):
        at = lax.rem(x + 4 - n, 4) * 4
        copies.append(
            (
                pltpu.make_async_copy(h_ref.at[pl.ds(at, 4)], h_buf.at[n], sems.at[n, 0]),
                pltpu.make_async_copy(w_refs[n], w_buf.at[n], sems.at[n, 1]),
            )
        )
        for copy in copies[n]:
            copy.start()
    total = None
    for n in range(4):
        for copy in copies[n]:
            copy.wait()
        a = jnp.concatenate([h_buf[n, i] for i in range(4)], axis=1)
        term = jnp.dot(a, w_buf[n], preferred_element_type=jnp.float32)
        total = term if total is None else total + term
    for sel in range(2):
        o_ref[sel] = total[sel * 192 : (sel + 1) * 192]


def attend_kernel(info_ref, q_ref, cos_ref, sin_ref, *refs):
    mine, other_ref, o_ref, buf, s_ref, sems = refs[:4], *refs[4:]
    rows = q_ref.shape[0]
    x, y, core = info_ref[0], info_ref[1], info_ref[2]
    size = mine[0].shape[0]

    def copies(i):
        other = other_ref.at[pl.ds(i * size, size)]
        return [
            pltpu.make_async_copy(mine[i], buf.at[i, core], sems.at[i, 0]),
            pltpu.make_async_copy(other, buf.at[i, 1 - core], sems.at[i, 1]),
        ]

    for i in range(4):

        @pl.when(x >= i)
        def _(i=i):
            for copy in copies(i):
                copy.start()

    sums = q_ref[...]
    q = sums * cos_ref[...] + pltpu.roll(sums, HD // 2, 1) * sin_ref[...]
    q = q.astype(jnp.bfloat16)

    def lanes(v, op):
        out = v[:, :HD]
        for i in range(1, v.shape[1] // HD):
            out = op(out, v[:, i * HD : (i + 1) * HD])
        return out

    def scores(k):
        return lax.dot_general(
            q, k, (((1,), (1,)), ((), ())), preferred_element_type=jnp.float32
        )

    for copy in copies(0):
        copy.wait()
    s = scores(buf[0, 0])
    qp = y * rows + lax.broadcasted_iota(jnp.int32, s.shape, 0)
    kp = lax.broadcasted_iota(jnp.int32, s.shape, 1)
    s = jnp.where(qp >= kp, s, -jnp.inf)
    s_ref[0] = s
    top = lanes(s, jnp.maximum)
    for i in range(1, 4):

        @pl.when(x >= i)
        def _(i=i):
            for copy in copies(i):
                copy.wait()

    def first_pass(i, top):
        s = scores(buf[i, 0])
        s_ref[i] = s
        return jnp.maximum(top, lanes(s, jnp.maximum))

    top = lax.fori_loop(1, x + 1, first_pass, top)
    top = jnp.max(top, axis=1, keepdims=True)
    scale = HD**-0.5 * math.log2(math.e)

    def second_pass(i, state):
        tot, acc = state
        e = jnp.exp2((s_ref[i] - top) * scale)
        return tot + lanes(e, jnp.add), acc + jnp.dot(
            e.astype(jnp.bfloat16), buf[i, 1], preferred_element_type=jnp.float32
        )

    zero = jnp.zeros((rows, HD), jnp.float32)
    tot, acc = lax.fori_loop(0, x + 1, second_pass, (zero, zero))
    o_ref[...] = (acc / jnp.sum(tot, axis=1, keepdims=True)).astype(o_ref.dtype)


def project(info, h, pieces):
    count, m, part = h.shape
    hbm = pl.BlockSpec(memory_space=pl.ANY)
    return pl.pallas_call(
        project_kernel,
        in_specs=[pl.BlockSpec(memory_space=pltpu.SMEM)] + [hbm] * 5,
        out_specs=pl.BlockSpec(memory_space=pltpu.VMEM),
        out_shape=jax.ShapeDtypeStruct((2, m // 2, HD), jnp.float32),
        scratch_shapes=[
            pltpu.VMEM((4, count // 4, m, part), jnp.bfloat16),
            pltpu.VMEM((4, count // 4 * part, HD), jnp.bfloat16),
            pltpu.SemaphoreType.DMA((4, 2)),
        ],
        compiler_params=pltpu.CompilerParams(vmem_limit_bytes=48 * 2**20),
        cost_estimate=pl.CostEstimate(
            flops=2 * m * count * part * HD,
            bytes_accessed=2 * count * part * (m + HD),
            transcendentals=0,
        ),
        name="project",
    )(info, h, *pieces)


def attend(info, sums, cosine, sine, mine, other):
    vm = pl.BlockSpec(memory_space=pltpu.VMEM)
    return pl.pallas_call(
        attend_kernel,
        in_specs=[pl.BlockSpec(memory_space=pltpu.SMEM), vm, vm, vm]
        + [pl.BlockSpec(memory_space=pl.ANY)] * 5,
        out_specs=vm,
        out_shape=jax.ShapeDtypeStruct(sums.shape, jnp.bfloat16),
        scratch_shapes=[
            pltpu.VMEM((4, 2, 1536, HD), jnp.bfloat16),
            pltpu.VMEM((4, 192, 1536), jnp.float32),
            pltpu.SemaphoreType.DMA((4, 2)),
        ],
        compiler_params=pltpu.CompilerParams(vmem_limit_bytes=40 * 2**20),
        cost_estimate=pl.CostEstimate(
            flops=4 * 192 * 6144 * HD,
            bytes_accessed=4 * 6144 * HD,
            transcendentals=192 * 6144,
        ),
        name="attend",
    )(info, sums, cosine, sine, *mine, other)


def shift(v, axis, by):
    n = lax.axis_size(axis)
    return lax.ppermute(v, axis, [(i, (i + by) % n) for i in range(n)])


def shift_up(v, axis, by):
    n = lax.axis_size(axis)
    return lax.ppermute(v, axis, [(i, i + by) for i in range(n - by)])


def swap(v, axis):
    return lax.ppermute(v, axis, [(0, 1), (1, 0)])


def body(hidden, query_weight, kv_weight):
    x, yq, yp, z, core = (lax.axis_index(a) for a in AXES)
    y = yq * 2 + yp
    base = (x * 8 + y) * 192
    info = jnp.stack([x, y, core])
    tie = lax.optimization_barrier

    w = lax.all_gather(query_weight, "yq", axis=0, tiled=True)

    (hs,) = small_kernel(slabs_kernel, "slabs", [(32, 12, 512)], (hidden,))
    hs = lax.all_to_all(hs, PAIR, 0, 0, tiled=True)
    h, part = mix(info, hs, kv_weight)
    h = lax.all_gather(h, TP, axis=0, tiled=False)

    part = lax.all_to_all(part, PAIR, 0, 0, tiled=True)
    up, down = shift(w, "x", 1), shift(w, "x", -1)
    rows = jnp.sum(part, axis=0)
    cosine, sine = angles_of(base + z * 24 + jnp.arange(24, dtype=jnp.int32))
    rows = jnp.where(core == 0, rotate(rows, cosine, sine), rows).astype(jnp.bfloat16)
    rows = broadcast_gather(rows, ("yq", "yp", "z")).reshape(1536, HD)
    first, last = small_kernel(ends_kernel, "ends", [(1024, HD)] * 2, (up, down))
    cross = [shift(first, "x", 1), shift(last, "x", -1)]
    rows, cross = tie((rows, cross))
    mine = [rows] + [shift_up(rows, "x", d) for d in (1, 2, 3)]

    sums = project(info, h, (w, up, jnp.concatenate(cross, axis=0), down))
    keep = jnp.where(yp == 0, sums[0], sums[1])
    come = swap(jnp.where(yp == 0, sums[1], sums[0]), "yp")
    away, sums = tie((mine[1:], sums))
    (other,) = small_kernel(join_kernel, "join", [(6144, HD)], (rows, *away))
    other = swap(other, "core")
    cosine, sine = angles_of(base + jnp.arange(192, dtype=jnp.int32))
    cosine = jnp.concatenate([cosine, cosine], axis=1)
    sine = jnp.concatenate([-sine, sine], axis=1)
    return attend(info, keep + come, cosine, sine, mine, other)


def solution(mesh):
    in_specs = (P(AXES, None), P(CTX, TP), P(TP, None))
    out_specs = P(CTX, TP)
    return jax.shard_map(
        body, mesh=fine_mesh(mesh), in_specs=in_specs, out_specs=out_specs, check_vma=False
    )
```

```python
import math

import jax
import jax.numpy as jnp
from jax import lax
from jax.experimental import pallas as pl
from jax.experimental.pallas import tpu as pltpu
from jax.sharding import Mesh
from jax.sharding import PartitionSpec as P

HD = 128
CTX = ("x", "yq", "yp")
TP = ("z", "core")
PAIR = ("yp", "z", "core")
AXES = CTX + TP


def fine_mesh(mesh):
    return Mesh(mesh.devices.reshape(4, 4, 2, 8, 2), AXES)


def angles_of(positions):
    half = HD // 2
    exponent = jnp.arange(half, dtype=jnp.float32) * (2.0 / HD)
    frequency = jnp.power(jnp.float32(500000.0), -exponent)
    angles = positions.astype(jnp.float32)[:, None] * frequency[None, :]
    return jnp.cos(angles), jnp.sin(angles)


def rotate(field, cosine, sine):
    half = HD // 2
    first, second = field[:, :half], field[:, half:]
    return jnp.concatenate(
        [first * cosine - second * sine, second * cosine + first * sine], axis=1
    )


def broadcast_gather(x, axis):
    n = lax.axis_size(axis)
    return lax.all_to_all(
        jnp.broadcast_to(x[None], (n,) + x.shape), axis, 0, 0, tiled=True
    )


def slabs_kernel(h_ref, o_ref):
    for yp in range(2):
        for t in range(16):
            at = (2 * t + yp) * 512
            o_ref[yp * 16 + t] = h_ref[:, at : at + 512]


def mix_kernel(info_ref, x_ref, w_ref, rows_ref, o_ref, buf):
    yp = lax.rem(info_ref[1], 2)
    for i in range(32):
        buf[i * 12 : (i + 1) * 12, :] = x_ref[i].astype(jnp.float32)
    rows = buf[...].astype(jnp.bfloat16)
    rows_ref[...] = rows
    w = w_ref[pl.ds(pl.multiple_of(yp * 512, 512), 512), :]
    sums = jnp.dot(rows, w, preferred_element_type=jnp.float32)
    for i in range(16):
        for k in range(2):
            o_ref[2 * i + k] = sums[i * 24 : (i + 1) * 24, k * HD : (k + 1) * HD]


def mix(info, x, w):
    vm = pl.BlockSpec(memory_space=pltpu.VMEM)
    return pl.pallas_call(
        mix_kernel,
        in_specs=[pl.BlockSpec(memory_space=pltpu.SMEM), vm, vm],
        out_specs=[vm, vm],
        out_shape=[
            jax.ShapeDtypeStruct((384, 512), jnp.bfloat16),
            jax.ShapeDtypeStruct((32, 24, HD), jnp.float32),
        ],
        scratch_shapes=[pltpu.VMEM((384, 512), jnp.float32)],
        compiler_params=pltpu.CompilerParams(vmem_limit_bytes=24 * 2**20),
        cost_estimate=pl.CostEstimate(
            flops=2 * 384 * 512 * 256, bytes_accessed=2**20, transcendentals=0
        ),
        name="mix",
    )(info, x, w)


def ends_kernel(up_ref, down_ref, first_ref, last_ref):
    part = first_ref.shape[0]
    first_ref[...] = up_ref[:part]
    last_ref[...] = down_ref[part:]


def join_kernel(*refs):
    size = refs[0].shape[0]
    for i, ref in enumerate(refs[:-1]):
        refs[-1][i * size : (i + 1) * size] = ref[...]


def small_kernel(kernel, name, outs, args):
    vm = pl.BlockSpec(memory_space=pltpu.VMEM)
    smem = pl.BlockSpec(memory_space=pltpu.SMEM)
    return pl.pallas_call(
        kernel,
        in_specs=[smem if a.ndim == 1 else vm for a in args],
        out_specs=[vm] * len(outs),
        out_shape=[jax.ShapeDtypeStruct(o, jnp.bfloat16) for o in outs],
        compiler_params=pltpu.CompilerParams(vmem_limit_bytes=24 * 2**20),
        cost_estimate=pl.CostEstimate(flops=0, bytes_accessed=2**20, transcendentals=0),
        name=name,
    )(*args)


def project_kernel(info_ref, h_ref, *refs):
    w_refs, o_ref, h_buf, w_buf, sems = refs[:4], *refs[4:]
    x, yq = info_ref[0], info_ref[1] // 2
    copies = []
    for n in range(4):
        group = [pltpu.make_async_copy(w_refs[n], w_buf.at[n], sems.at[n, 4])]
        for back in range(4):
            block = lax.rem(x + 4 - n, 4) * 4 + lax.rem(yq + 4 - back, 4)
            group.append(
                pltpu.make_async_copy(h_ref.at[block], h_buf.at[n, back], sems.at[n, back])
            )
        copies.append(group)
        for copy in group:
            copy.start()
    total = None
    for n in range(4):
        for copy in copies[n]:
            copy.wait()
        a = jnp.concatenate([h_buf[n, i] for i in range(4)], axis=1)
        term = jnp.dot(a, w_buf[n], preferred_element_type=jnp.float32)
        total = term if total is None else total + term
    for sel in range(2):
        o_ref[sel] = total[sel * 192 : (sel + 1) * 192]


def attend_kernel(info_ref, q_ref, cos_ref, sin_ref, *refs):
    mine, other_ref, o_ref, buf, s_ref, sems = refs[:4], *refs[4:]
    rows = q_ref.shape[0]
    x, y, core = info_ref[0], info_ref[1], info_ref[2]
    size = mine[0].shape[0]

    def copies(i):
        other = other_ref.at[pl.ds(i * size, size)]
        return [
            pltpu.make_async_copy(mine[i], buf.at[i, core], sems.at[i, 0]),
            pltpu.make_async_copy(other, buf.at[i, 1 - core], sems.at[i, 1]),
        ]

    for i in range(4):

        @pl.when(x >= i)
        def _(i=i):
            for copy in copies(i):
                copy.start()

    sums = q_ref[...]
    q = sums * cos_ref[...] + pltpu.roll(sums, HD // 2, 1) * sin_ref[...]
    q = q.astype(jnp.bfloat16)

    def lanes(v, op):
        out = v[:, :HD]
        for i in range(1, v.shape[1] // HD):
            out = op(out, v[:, i * HD : (i + 1) * HD])
        return out

    def scores(k):
        return lax.dot_general(
            q, k, (((1,), (1,)), ((), ())), preferred_element_type=jnp.float32
        )

    for copy in copies(0):
        copy.wait()
    s = scores(buf[0, 0])
    qp = y * rows + lax.broadcasted_iota(jnp.int32, s.shape, 0)
    kp = lax.broadcasted_iota(jnp.int32, s.shape, 1)
    s = jnp.where(qp >= kp, s, -jnp.inf)
    s_ref[0] = s
    top = lanes(s, jnp.maximum)
    for i in range(1, 4):

        @pl.when(x >= i)
        def _(i=i):
            for copy in copies(i):
                copy.wait()

    def first_pass(i, top):
        s = scores(buf[i, 0])
        s_ref[i] = s
        return jnp.maximum(top, lanes(s, jnp.maximum))

    top = lax.fori_loop(1, x + 1, first_pass, top)
    top = jnp.max(top, axis=1, keepdims=True)
    scale = HD**-0.5 * math.log2(math.e)

    def second_pass(i, state):
        tot, acc = state
        e = jnp.exp2((s_ref[i] - top) * scale)
        return tot + lanes(e, jnp.add), acc + jnp.dot(
            e.astype(jnp.bfloat16), buf[i, 1], preferred_element_type=jnp.float32
        )

    zero = jnp.zeros((rows, HD), jnp.float32)
    tot, acc = lax.fori_loop(0, x + 1, second_pass, (zero, zero))
    o_ref[...] = (acc / jnp.sum(tot, axis=1, keepdims=True)).astype(o_ref.dtype)


def project(info, h, pieces):
    count, m, part = h.shape
    hbm = pl.BlockSpec(memory_space=pl.ANY)
    return pl.pallas_call(
        project_kernel,
        in_specs=[pl.BlockSpec(memory_space=pltpu.SMEM)] + [hbm] * 5,
        out_specs=pl.BlockSpec(memory_space=pltpu.VMEM),
        out_shape=jax.ShapeDtypeStruct((2, m // 2, HD), jnp.float32),
        scratch_shapes=[
            pltpu.VMEM((4, count // 4, m, part), jnp.bfloat16),
            pltpu.VMEM((4, count // 4 * part, HD), jnp.bfloat16),
            pltpu.SemaphoreType.DMA((4, 5)),
        ],
        compiler_params=pltpu.CompilerParams(vmem_limit_bytes=48 * 2**20),
        cost_estimate=pl.CostEstimate(
            flops=2 * m * count * part * HD,
            bytes_accessed=2 * count * part * (m + HD),
            transcendentals=0,
        ),
        name="project",
    )(info, h, *pieces)


def attend(info, sums, cosine, sine, mine, other):
    vm = pl.BlockSpec(memory_space=pltpu.VMEM)
    return pl.pallas_call(
        attend_kernel,
        in_specs=[pl.BlockSpec(memory_space=pltpu.SMEM), vm, vm, vm]
        + [pl.BlockSpec(memory_space=pl.ANY)] * 5,
        out_specs=vm,
        out_shape=jax.ShapeDtypeStruct(sums.shape, jnp.bfloat16),
        scratch_shapes=[
            pltpu.VMEM((4, 2, 1536, HD), jnp.bfloat16),
            pltpu.VMEM((4, 192, 1536), jnp.float32),
            pltpu.SemaphoreType.DMA((4, 2)),
        ],
        compiler_params=pltpu.CompilerParams(vmem_limit_bytes=40 * 2**20),
        cost_estimate=pl.CostEstimate(
            flops=4 * 192 * 6144 * HD,
            bytes_accessed=4 * 6144 * HD,
            transcendentals=192 * 6144,
        ),
        name="attend",
    )(info, sums, cosine, sine, *mine, other)


def shift(v, axis, by):
    n = lax.axis_size(axis)
    return lax.ppermute(v, axis, [(i, (i + by) % n) for i in range(n)])


def shift_up(v, axis, by):
    n = lax.axis_size(axis)
    return lax.ppermute(v, axis, [(i, i + by) for i in range(n - by)])


def swap(v, axis):
    return lax.ppermute(v, axis, [(0, 1), (1, 0)])


def body(hidden, query_weight, kv_weight):
    x, yq, yp, z, core = (lax.axis_index(a) for a in AXES)
    y = yq * 2 + yp
    base = (x * 8 + y) * 192
    info = jnp.stack([x, y, core])
    tie = lax.optimization_barrier

    (hs,) = small_kernel(slabs_kernel, "slabs", [(32, 12, 512)], (hidden,))
    hs, w = tie((hs, query_weight))
    hs = lax.all_to_all(hs, PAIR, 0, 0, tiled=True)

    w = [w] + [shift(w, "yq", d) for d in (1, 2, 3)]
    hs, w = tie((hs, w))
    h, part = mix(info, hs, kv_weight)
    h = lax.all_gather(h, TP, axis=0, tiled=False)
    w = jnp.concatenate(w, axis=0)

    part = lax.all_to_all(part, PAIR, 0, 0, tiled=True)
    up, down = shift(w, "x", 1), shift(w, "x", -1)
    rows = jnp.sum(part, axis=0)
    cosine, sine = angles_of(base + z * 24 + jnp.arange(24, dtype=jnp.int32))
    rows = jnp.where(core == 0, rotate(rows, cosine, sine), rows).astype(jnp.bfloat16)
    rows = broadcast_gather(rows, ("yq", "yp", "z")).reshape(1536, HD)
    first, last = small_kernel(ends_kernel, "ends", [(1024, HD)] * 2, (up, down))
    cross = [shift(first, "x", 1), shift(last, "x", -1)]
    rows, cross = tie((rows, cross))
    mine = [rows] + [shift_up(rows, "x", d) for d in (1, 2, 3)]

    sums = project(info, h, (w, up, jnp.concatenate(cross, axis=0), down))
    keep = jnp.where(yp == 0, sums[0], sums[1])
    come = swap(jnp.where(yp == 0, sums[1], sums[0]), "yp")
    away, come = tie((mine[1:], come))
    (other,) = small_kernel(join_kernel, "join", [(6144, HD)], (rows, *away))
    other = swap(other, "core")
    cosine, sine = angles_of(base + jnp.arange(192, dtype=jnp.int32))
    cosine = jnp.concatenate([cosine, cosine], axis=1)
    sine = jnp.concatenate([-sine, sine], axis=1)
    return attend(info, keep + come, cosine, sine, mine, other)


def solution(mesh):
    in_specs = (P(AXES, None), P(CTX, TP), P(TP, None))
    out_specs = P(CTX, TP)
    return jax.shard_map(
        body, mesh=fine_mesh(mesh), in_specs=in_specs, out_specs=out_specs, check_vma=False
    )
```

```python
import math

import jax
import jax.numpy as jnp
from jax import lax
from jax.experimental import pallas as pl
from jax.experimental.pallas import tpu as pltpu
from jax.sharding import Mesh
from jax.sharding import PartitionSpec as P

HD = 128
CTX = ("x", "yq", "yp")
TP = ("z", "core")
PAIR = ("yp", "z", "core")
AXES = CTX + TP


def fine_mesh(mesh):
    return Mesh(mesh.devices.reshape(4, 4, 2, 8, 2), AXES)


def angles_of(positions):
    half = HD // 2
    exponent = jnp.arange(half, dtype=jnp.float32) * (2.0 / HD)
    frequency = jnp.power(jnp.float32(500000.0), -exponent)
    angles = positions.astype(jnp.float32)[:, None] * frequency[None, :]
    return jnp.cos(angles), jnp.sin(angles)


def rotate(field, cosine, sine):
    half = HD // 2
    first, second = field[:, :half], field[:, half:]
    return jnp.concatenate(
        [first * cosine - second * sine, second * cosine + first * sine], axis=1
    )


def broadcast_gather(x, axis):
    n = lax.axis_size(axis)
    return lax.all_to_all(
        jnp.broadcast_to(x[None], (n,) + x.shape), axis, 0, 0, tiled=True
    )


def slabs_kernel(h_ref, o_ref):
    for yp in range(2):
        for t in range(16):
            at = (2 * t + yp) * 512
            o_ref[yp * 16 + t] = h_ref[:, at : at + 512]


def mix_kernel(info_ref, x_ref, w_ref, rows_ref, o_ref, buf):
    yp = lax.rem(info_ref[1], 2)
    for i in range(32):
        buf[i * 12 : (i + 1) * 12, :] = x_ref[i].astype(jnp.float32)
    rows = buf[...].astype(jnp.bfloat16)
    rows_ref[...] = rows
    w = w_ref[pl.ds(pl.multiple_of(yp * 512, 512), 512), :]
    sums = jnp.dot(rows, w, preferred_element_type=jnp.float32)
    for i in range(16):
        for k in range(2):
            o_ref[2 * i + k] = sums[i * 24 : (i + 1) * 24, k * HD : (k + 1) * HD]


def mix(info, x, w):
    vm = pl.BlockSpec(memory_space=pltpu.VMEM)
    return pl.pallas_call(
        mix_kernel,
        in_specs=[pl.BlockSpec(memory_space=pltpu.SMEM), vm, vm],
        out_specs=[vm, vm],
        out_shape=[
            jax.ShapeDtypeStruct((384, 512), jnp.bfloat16),
            jax.ShapeDtypeStruct((32, 24, HD), jnp.float32),
        ],
        scratch_shapes=[pltpu.VMEM((384, 512), jnp.float32)],
        compiler_params=pltpu.CompilerParams(vmem_limit_bytes=24 * 2**20),
        cost_estimate=pl.CostEstimate(
            flops=2 * 384 * 512 * 256, bytes_accessed=2**20, transcendentals=0
        ),
        name="mix",
    )(info, x, w)


def ends_kernel(up_ref, down_ref, first_ref, last_ref):
    part = first_ref.shape[0]
    first_ref[...] = up_ref[:part]
    last_ref[...] = down_ref[part:]


def join_kernel(*refs):
    size = refs[0].shape[0]
    for i, ref in enumerate(refs[:-1]):
        refs[-1][i * size : (i + 1) * size] = ref[...]


def small_kernel(kernel, name, outs, args):
    vm = pl.BlockSpec(memory_space=pltpu.VMEM)
    smem = pl.BlockSpec(memory_space=pltpu.SMEM)
    return pl.pallas_call(
        kernel,
        in_specs=[smem if a.ndim == 1 else vm for a in args],
        out_specs=[vm] * len(outs),
        out_shape=[jax.ShapeDtypeStruct(o, jnp.bfloat16) for o in outs],
        compiler_params=pltpu.CompilerParams(vmem_limit_bytes=24 * 2**20),
        cost_estimate=pl.CostEstimate(flops=0, bytes_accessed=2**20, transcendentals=0),
        name=name,
    )(*args)


def project_kernel(info_ref, h_ref, *refs):
    w_refs, o_ref, h_buf, w_buf, sems = refs[:4], *refs[4:]
    x, yq = info_ref[0], info_ref[1] // 2
    copies = []
    for n in range(4):
        group = [pltpu.make_async_copy(w_refs[n], w_buf.at[n], sems.at[n, 4])]
        for back in range(4):
            block = lax.rem(x + 4 - n, 4) * 4 + lax.rem(yq + 4 - back, 4)
            group.append(
                pltpu.make_async_copy(h_ref.at[block], h_buf.at[n, back], sems.at[n, back])
            )
        copies.append(group)
        for copy in group:
            copy.start()
    total = None
    for n in range(4):
        for copy in copies[n]:
            copy.wait()
        a = jnp.concatenate([h_buf[n, i] for i in range(4)], axis=1)
        term = jnp.dot(a, w_buf[n], preferred_element_type=jnp.float32)
        total = term if total is None else total + term
    for sel in range(2):
        o_ref[sel] = total[sel * 192 : (sel + 1) * 192]


def attend_kernel(info_ref, q_ref, cos_ref, sin_ref, *refs):
    mine, other_ref, o_ref, buf, s_ref, sems = refs[:4], *refs[4:]
    rows = q_ref.shape[0]
    x, y, core = info_ref[0], info_ref[1], info_ref[2]
    size = mine[0].shape[0]

    def copies(i):
        other = other_ref.at[pl.ds(i * size, size)]
        return [
            pltpu.make_async_copy(mine[i], buf.at[i, core], sems.at[i, 0]),
            pltpu.make_async_copy(other, buf.at[i, 1 - core], sems.at[i, 1]),
        ]

    for i in range(4):

        @pl.when(x >= i)
        def _(i=i):
            for copy in copies(i):
                copy.start()

    sums = q_ref[...]
    q = sums * cos_ref[...] + pltpu.roll(sums, HD // 2, 1) * sin_ref[...]
    q = q.astype(jnp.bfloat16)

    def lanes(v, op):
        out = v[:, :HD]
        for i in range(1, v.shape[1] // HD):
            out = op(out, v[:, i * HD : (i + 1) * HD])
        return out

    def scores(k):
        return lax.dot_general(
            q, k, (((1,), (1,)), ((), ())), preferred_element_type=jnp.float32
        )

    for copy in copies(0):
        copy.wait()
    s = scores(buf[0, 0])
    qp = y * rows + lax.broadcasted_iota(jnp.int32, s.shape, 0)
    kp = lax.broadcasted_iota(jnp.int32, s.shape, 1)
    s = jnp.where(qp >= kp, s, -jnp.inf)
    s_ref[0] = s
    top = lanes(s, jnp.maximum)
    for i in range(1, 4):

        @pl.when(x >= i)
        def _(i=i):
            for copy in copies(i):
                copy.wait()

    def first_pass(i, top):
        s = scores(buf[i, 0])
        s_ref[i] = s
        return jnp.maximum(top, lanes(s, jnp.maximum))

    top = lax.fori_loop(1, x + 1, first_pass, top)
    top = jnp.max(top, axis=1, keepdims=True)
    scale = HD**-0.5 * math.log2(math.e)

    def second_pass(i, state):
        tot, acc = state
        e = jnp.exp2((s_ref[i] - top) * scale)
        return tot + lanes(e, jnp.add), acc + jnp.dot(
            e.astype(jnp.bfloat16), buf[i, 1], preferred_element_type=jnp.float32
        )

    zero = jnp.zeros((rows, HD), jnp.float32)
    tot, acc = lax.fori_loop(0, x + 1, second_pass, (zero, zero))
    o_ref[...] = (acc / jnp.sum(tot, axis=1, keepdims=True)).astype(o_ref.dtype)


def project(info, h, pieces):
    count, m, part = h.shape
    hbm = pl.BlockSpec(memory_space=pl.ANY)
    return pl.pallas_call(
        project_kernel,
        in_specs=[pl.BlockSpec(memory_space=pltpu.SMEM)] + [hbm] * 5,
        out_specs=pl.BlockSpec(memory_space=pltpu.VMEM),
        out_shape=jax.ShapeDtypeStruct((2, m // 2, HD), jnp.float32),
        scratch_shapes=[
            pltpu.VMEM((4, count // 4, m, part), jnp.bfloat16),
            pltpu.VMEM((4, count // 4 * part, HD), jnp.bfloat16),
            pltpu.SemaphoreType.DMA((4, 5)),
        ],
        compiler_params=pltpu.CompilerParams(vmem_limit_bytes=48 * 2**20),
        cost_estimate=pl.CostEstimate(
            flops=2 * m * count * part * HD,
            bytes_accessed=2 * count * part * (m + HD),
            transcendentals=0,
        ),
        name="project",
    )(info, h, *pieces)


def attend(info, sums, cosine, sine, mine, other):
    vm = pl.BlockSpec(memory_space=pltpu.VMEM)
    return pl.pallas_call(
        attend_kernel,
        in_specs=[pl.BlockSpec(memory_space=pltpu.SMEM), vm, vm, vm]
        + [pl.BlockSpec(memory_space=pl.ANY)] * 5,
        out_specs=vm,
        out_shape=jax.ShapeDtypeStruct(sums.shape, jnp.bfloat16),
        scratch_shapes=[
            pltpu.VMEM((4, 2, 1536, HD), jnp.bfloat16),
            pltpu.VMEM((4, 192, 1536), jnp.float32),
            pltpu.SemaphoreType.DMA((4, 2)),
        ],
        compiler_params=pltpu.CompilerParams(vmem_limit_bytes=40 * 2**20),
        cost_estimate=pl.CostEstimate(
            flops=4 * 192 * 6144 * HD,
            bytes_accessed=4 * 6144 * HD,
            transcendentals=192 * 6144,
        ),
        name="attend",
    )(info, sums, cosine, sine, *mine, other)


def shift(v, axis, by):
    n = lax.axis_size(axis)
    return lax.ppermute(v, axis, [(i, (i + by) % n) for i in range(n)])


def shift_up(v, axis, by):
    n = lax.axis_size(axis)
    return lax.ppermute(v, axis, [(i, i + by) for i in range(n - by)])


def swap(v, axis):
    return lax.ppermute(v, axis, [(0, 1), (1, 0)])


def body(hidden, query_weight, kv_weight):
    x, yq, yp, z, core = (lax.axis_index(a) for a in AXES)
    y = yq * 2 + yp
    base = (x * 8 + y) * 192
    info = jnp.stack([x, y, core])
    tie = lax.optimization_barrier

    (hs,) = small_kernel(slabs_kernel, "slabs", [(32, 12, 512)], (hidden,))
    hs, w = tie((hs, query_weight))
    hs = lax.all_to_all(hs, PAIR, 0, 0, tiled=True)

    one, three = shift(w, "yq", 1), shift(w, "yq", 3)
    hs, w, one, three = tie((hs, w, one, three))
    h, part = mix(info, hs, kv_weight)
    h = lax.all_gather(h, TP, axis=0, tiled=False)
    w = jnp.concatenate([w, one, shift(w, "yq", 2), three], axis=0)

    part = lax.all_to_all(part, PAIR, 0, 0, tiled=True)
    up, down = shift(w, "x", 1), shift(w, "x", -1)
    rows = jnp.sum(part, axis=0)
    cosine, sine = angles_of(base + z * 24 + jnp.arange(24, dtype=jnp.int32))
    rows = jnp.where(core == 0, rotate(rows, cosine, sine), rows).astype(jnp.bfloat16)
    rows = broadcast_gather(rows, ("yq", "yp", "z")).reshape(1536, HD)
    first, last = small_kernel(ends_kernel, "ends", [(1024, HD)] * 2, (up, down))
    cross = [shift(first, "x", 1), shift(last, "x", -1)]
    rows, cross = tie((rows, cross))
    mine = [rows] + [shift_up(rows, "x", d) for d in (1, 2, 3)]

    sums = project(info, h, (w, up, jnp.concatenate(cross, axis=0), down))
    keep = jnp.where(yp == 0, sums[0], sums[1])
    come = swap(jnp.where(yp == 0, sums[1], sums[0]), "yp")
    away, come = tie((mine[1:], come))
    (other,) = small_kernel(join_kernel, "join", [(6144, HD)], (rows, *away))
    other = swap(other, "core")
    cosine, sine = angles_of(base + jnp.arange(192, dtype=jnp.int32))
    cosine = jnp.concatenate([cosine, cosine], axis=1)
    sine = jnp.concatenate([-sine, sine], axis=1)
    return attend(info, keep + come, cosine, sine, mine, other)


def solution(mesh):
    in_specs = (P(AXES, None), P(CTX, TP), P(TP, None))
    out_specs = P(CTX, TP)
    return jax.shard_map(
        body, mesh=fine_mesh(mesh), in_specs=in_specs, out_specs=out_specs, check_vma=False
    )
```

```python
import math

import jax
import jax.numpy as jnp
from jax import lax
from jax.experimental import pallas as pl
from jax.experimental.pallas import tpu as pltpu
from jax.sharding import Mesh
from jax.sharding import PartitionSpec as P

HD = 128
CTX = ("x", "yq", "yp")
TP = ("z", "core")
PAIR = ("yp", "z", "core")
AXES = CTX + TP


def fine_mesh(mesh):
    return Mesh(mesh.devices.reshape(4, 4, 2, 8, 2), AXES)


def angles_of(positions):
    half = HD // 2
    exponent = jnp.arange(half, dtype=jnp.float32) * (2.0 / HD)
    frequency = jnp.power(jnp.float32(500000.0), -exponent)
    angles = positions.astype(jnp.float32)[:, None] * frequency[None, :]
    return jnp.cos(angles), jnp.sin(angles)


def rotate(field, cosine, sine):
    half = HD // 2
    first, second = field[:, :half], field[:, half:]
    return jnp.concatenate(
        [first * cosine - second * sine, second * cosine + first * sine], axis=1
    )


def broadcast_gather(x, axis):
    n = lax.axis_size(axis)
    return lax.all_to_all(
        jnp.broadcast_to(x[None], (n,) + x.shape), axis, 0, 0, tiled=True
    )


def slabs_kernel(h_ref, o_ref):
    for yp in range(2):
        for t in range(16):
            at = (2 * t + yp) * 512
            o_ref[yp * 16 + t] = h_ref[:, at : at + 512]


def mix_kernel(info_ref, x_ref, w_ref, rows_ref, o_ref, buf):
    yp = lax.rem(info_ref[1], 2)
    for i in range(32):
        buf[i * 12 : (i + 1) * 12, :] = x_ref[i].astype(jnp.float32)
    rows = buf[...].astype(jnp.bfloat16)
    rows_ref[...] = rows
    w = w_ref[pl.ds(pl.multiple_of(yp * 512, 512), 512), :]
    sums = jnp.dot(rows, w, preferred_element_type=jnp.float32)
    for i in range(16):
        for k in range(2):
            o_ref[2 * i + k] = sums[i * 24 : (i + 1) * 24, k * HD : (k + 1) * HD]


def mix(info, x, w):
    vm = pl.BlockSpec(memory_space=pltpu.VMEM)
    return pl.pallas_call(
        mix_kernel,
        in_specs=[pl.BlockSpec(memory_space=pltpu.SMEM), vm, vm],
        out_specs=[vm, vm],
        out_shape=[
            jax.ShapeDtypeStruct((384, 512), jnp.bfloat16),
            jax.ShapeDtypeStruct((32, 24, HD), jnp.float32),
        ],
        scratch_shapes=[pltpu.VMEM((384, 512), jnp.float32)],
        compiler_params=pltpu.CompilerParams(vmem_limit_bytes=24 * 2**20),
        cost_estimate=pl.CostEstimate(
            flops=2 * 384 * 512 * 256, bytes_accessed=2**20, transcendentals=0
        ),
        name="mix",
    )(info, x, w)


def ends_kernel(up_ref, down_ref, first_ref, last_ref):
    part = first_ref.shape[0]
    first_ref[...] = up_ref[:part]
    last_ref[...] = down_ref[part:]


def join_kernel(*refs):
    size = refs[0].shape[0]
    for i, ref in enumerate(refs[:-1]):
        refs[-1][i * size : (i + 1) * size] = ref[...]


def small_kernel(kernel, name, outs, args):
    vm = pl.BlockSpec(memory_space=pltpu.VMEM)
    smem = pl.BlockSpec(memory_space=pltpu.SMEM)
    return pl.pallas_call(
        kernel,
        in_specs=[smem if a.ndim == 1 else vm for a in args],
        out_specs=[vm] * len(outs),
        out_shape=[jax.ShapeDtypeStruct(o, jnp.bfloat16) for o in outs],
        compiler_params=pltpu.CompilerParams(vmem_limit_bytes=24 * 2**20),
        cost_estimate=pl.CostEstimate(flops=0, bytes_accessed=2**20, transcendentals=0),
        name=name,
    )(*args)


def project_kernel(info_ref, h_ref, *refs):
    w_refs, o_ref, h_buf, w_buf, sems = refs[:4], *refs[4:]
    x, yq = info_ref[0], info_ref[1] // 2
    copies = []
    for n in range(4):
        group = [pltpu.make_async_copy(w_refs[n], w_buf.at[n], sems.at[n, 4])]
        for back in range(4):
            block = lax.rem(x + 4 - n, 4) * 4 + lax.rem(yq + 4 - back, 4)
            group.append(
                pltpu.make_async_copy(h_ref.at[block], h_buf.at[n, back], sems.at[n, back])
            )
        copies.append(group)
        for copy in group:
            copy.start()
    total = None
    for n in range(4):
        for copy in copies[n]:
            copy.wait()
        a = jnp.concatenate([h_buf[n, i] for i in range(4)], axis=1)
        term = jnp.dot(a, w_buf[n], preferred_element_type=jnp.float32)
        total = term if total is None else total + term
    for sel in range(2):
        o_ref[sel] = total[sel * 192 : (sel + 1) * 192]


def attend_kernel(info_ref, q_ref, cos_ref, sin_ref, *refs):
    mine, other_ref, o_ref, buf, s_ref, sems = refs[:4], *refs[4:]
    rows = q_ref.shape[0]
    x, y, core = info_ref[0], info_ref[1], info_ref[2]
    size = mine[0].shape[0]

    def copies(i):
        other = other_ref.at[pl.ds(i * size, size)]
        return [
            pltpu.make_async_copy(mine[i], buf.at[i, core], sems.at[i, 0]),
            pltpu.make_async_copy(other, buf.at[i, 1 - core], sems.at[i, 1]),
        ]

    for i in range(4):

        @pl.when(x >= i)
        def _(i=i):
            for copy in copies(i):
                copy.start()

    sums = q_ref[...]
    q = sums * cos_ref[...] + pltpu.roll(sums, HD // 2, 1) * sin_ref[...]
    q = q.astype(jnp.bfloat16)

    def lanes(v, op):
        out = v[:, :HD]
        for i in range(1, v.shape[1] // HD):
            out = op(out, v[:, i * HD : (i + 1) * HD])
        return out

    def scores(k):
        return lax.dot_general(
            q, k, (((1,), (1,)), ((), ())), preferred_element_type=jnp.float32
        )

    for copy in copies(0):
        copy.wait()
    s = scores(buf[0, 0])
    qp = y * rows + lax.broadcasted_iota(jnp.int32, s.shape, 0)
    kp = lax.broadcasted_iota(jnp.int32, s.shape, 1)
    s = jnp.where(qp >= kp, s, -jnp.inf)
    s_ref[0] = s
    top = lanes(s, jnp.maximum)
    for i in range(1, 4):

        @pl.when(x >= i)
        def _(i=i):
            for copy in copies(i):
                copy.wait()

    def first_pass(i, top):
        s = scores(buf[i, 0])
        s_ref[i] = s
        return jnp.maximum(top, lanes(s, jnp.maximum))

    top = lax.fori_loop(1, x + 1, first_pass, top)
    top = jnp.max(top, axis=1, keepdims=True)
    scale = HD**-0.5 * math.log2(math.e)

    def second_pass(i, state):
        tot, acc = state
        e = jnp.exp2((s_ref[i] - top) * scale)
        return tot + lanes(e, jnp.add), acc + jnp.dot(
            e.astype(jnp.bfloat16), buf[i, 1], preferred_element_type=jnp.float32
        )

    zero = jnp.zeros((rows, HD), jnp.float32)
    tot, acc = lax.fori_loop(0, x + 1, second_pass, (zero, zero))
    o_ref[...] = (acc / jnp.sum(tot, axis=1, keepdims=True)).astype(o_ref.dtype)


def project(info, h, pieces):
    count, m, part = h.shape
    hbm = pl.BlockSpec(memory_space=pl.ANY)
    return pl.pallas_call(
        project_kernel,
        in_specs=[pl.BlockSpec(memory_space=pltpu.SMEM)] + [hbm] * 5,
        out_specs=pl.BlockSpec(memory_space=pltpu.VMEM),
        out_shape=jax.ShapeDtypeStruct((2, m // 2, HD), jnp.float32),
        scratch_shapes=[
            pltpu.VMEM((4, count // 4, m, part), jnp.bfloat16),
            pltpu.VMEM((4, count // 4 * part, HD), jnp.bfloat16),
            pltpu.SemaphoreType.DMA((4, 5)),
        ],
        compiler_params=pltpu.CompilerParams(vmem_limit_bytes=48 * 2**20),
        cost_estimate=pl.CostEstimate(
            flops=2 * m * count * part * HD,
            bytes_accessed=2 * count * part * (m + HD),
            transcendentals=0,
        ),
        name="project",
    )(info, h, *pieces)


def attend(info, sums, cosine, sine, mine, other):
    vm = pl.BlockSpec(memory_space=pltpu.VMEM)
    return pl.pallas_call(
        attend_kernel,
        in_specs=[pl.BlockSpec(memory_space=pltpu.SMEM), vm, vm, vm]
        + [pl.BlockSpec(memory_space=pl.ANY)] * 5,
        out_specs=vm,
        out_shape=jax.ShapeDtypeStruct(sums.shape, jnp.bfloat16),
        scratch_shapes=[
            pltpu.VMEM((4, 2, 1536, HD), jnp.bfloat16),
            pltpu.VMEM((4, 192, 1536), jnp.float32),
            pltpu.SemaphoreType.DMA((4, 2)),
        ],
        compiler_params=pltpu.CompilerParams(vmem_limit_bytes=40 * 2**20),
        cost_estimate=pl.CostEstimate(
            flops=4 * 192 * 6144 * HD,
            bytes_accessed=4 * 6144 * HD,
            transcendentals=192 * 6144,
        ),
        name="attend",
    )(info, sums, cosine, sine, *mine, other)


def shift(v, axis, by):
    n = lax.axis_size(axis)
    return lax.ppermute(v, axis, [(i, (i + by) % n) for i in range(n)])


def shift_up(v, axis, by):
    n = lax.axis_size(axis)
    return lax.ppermute(v, axis, [(i, i + by) for i in range(n - by)])


def swap(v, axis):
    return lax.ppermute(v, axis, [(0, 1), (1, 0)])


def body(hidden, query_weight, kv_weight):
    x, yq, yp, z, core = (lax.axis_index(a) for a in AXES)
    y = yq * 2 + yp
    base = (x * 8 + y) * 192
    info = jnp.stack([x, y, core])
    tie = lax.optimization_barrier

    (hs,) = small_kernel(slabs_kernel, "slabs", [(32, 12, 512)], (hidden,))
    hs, w = tie((hs, query_weight))
    hs = lax.all_to_all(hs, PAIR, 0, 0, tiled=True)

    one, three = shift(w, "yq", 1), shift(w, "yq", 3)
    hs, w, one, three = tie((hs, w, one, three))
    h, part = mix(info, hs, kv_weight)
    h = lax.all_gather(h, TP, axis=0, tiled=False)
    w = jnp.concatenate([w, one, shift(one, "yq", 1), three], axis=0)

    part = lax.all_to_all(part, PAIR, 0, 0, tiled=True)
    up, down = shift(w, "x", 1), shift(w, "x", -1)
    rows = jnp.sum(part, axis=0)
    cosine, sine = angles_of(base + z * 24 + jnp.arange(24, dtype=jnp.int32))
    rows = jnp.where(core == 0, rotate(rows, cosine, sine), rows).astype(jnp.bfloat16)
    rows = broadcast_gather(rows, ("yq", "yp", "z")).reshape(1536, HD)
    first, last = small_kernel(ends_kernel, "ends", [(1024, HD)] * 2, (up, down))
    cross = [shift(first, "x", 1), shift(last, "x", -1)]
    rows, cross = tie((rows, cross))
    mine = [rows] + [shift_up(rows, "x", d) for d in (1, 2, 3)]

    sums = project(info, h, (w, up, jnp.concatenate(cross, axis=0), down))
    keep = jnp.where(yp == 0, sums[0], sums[1])
    come = swap(jnp.where(yp == 0, sums[1], sums[0]), "yp")
    away, come = tie((mine[1:], come))
    (other,) = small_kernel(join_kernel, "join", [(6144, HD)], (rows, *away))
    other = swap(other, "core")
    cosine, sine = angles_of(base + jnp.arange(192, dtype=jnp.int32))
    cosine = jnp.concatenate([cosine, cosine], axis=1)
    sine = jnp.concatenate([-sine, sine], axis=1)
    return attend(info, keep + come, cosine, sine, mine, other)


def solution(mesh):
    in_specs = (P(AXES, None), P(CTX, TP), P(TP, None))
    out_specs = P(CTX, TP)
    return jax.shard_map(
        body, mesh=fine_mesh(mesh), in_specs=in_specs, out_specs=out_specs, check_vma=False
    )
```

```python
import math

import jax
import jax.numpy as jnp
from jax import lax
from jax.experimental import pallas as pl
from jax.experimental.pallas import tpu as pltpu
from jax.sharding import Mesh
from jax.sharding import PartitionSpec as P

HD = 128
CTX = ("x", "yq", "yp")
TP = ("z", "core")
PAIR = ("yp", "z", "core")
AXES = CTX + TP


def fine_mesh(mesh):
    return Mesh(mesh.devices.reshape(4, 4, 2, 8, 2), AXES)


def angles_of(positions):
    half = HD // 2
    exponent = jnp.arange(half, dtype=jnp.float32) * (2.0 / HD)
    frequency = jnp.power(jnp.float32(500000.0), -exponent)
    angles = positions.astype(jnp.float32)[:, None] * frequency[None, :]
    return jnp.cos(angles), jnp.sin(angles)


def rotate(field, cosine, sine):
    half = HD // 2
    first, second = field[:, :half], field[:, half:]
    return jnp.concatenate(
        [first * cosine - second * sine, second * cosine + first * sine], axis=1
    )


def broadcast_gather(x, axis):
    n = lax.axis_size(axis)
    return lax.all_to_all(
        jnp.broadcast_to(x[None], (n,) + x.shape), axis, 0, 0, tiled=True
    )


def slabs_kernel(h_ref, o_ref):
    for yp in range(2):
        for t in range(16):
            at = (2 * t + yp) * 512
            o_ref[yp * 16 + t] = h_ref[:, at : at + 512]


def mix_kernel(info_ref, x_ref, w_ref, rows_ref, o_ref, buf):
    yp = lax.rem(info_ref[1], 2)
    for i in range(32):
        buf[i * 12 : (i + 1) * 12, :] = x_ref[i].astype(jnp.float32)
    rows = buf[...].astype(jnp.bfloat16)
    rows_ref[...] = rows
    w = w_ref[pl.ds(pl.multiple_of(yp * 512, 512), 512), :]
    sums = jnp.dot(rows, w, preferred_element_type=jnp.float32)
    for i in range(16):
        for k in range(2):
            o_ref[2 * i + k] = sums[i * 24 : (i + 1) * 24, k * HD : (k + 1) * HD]


def mix(info, x, w):
    vm = pl.BlockSpec(memory_space=pltpu.VMEM)
    return pl.pallas_call(
        mix_kernel,
        in_specs=[pl.BlockSpec(memory_space=pltpu.SMEM), vm, vm],
        out_specs=[vm, vm],
        out_shape=[
            jax.ShapeDtypeStruct((384, 512), jnp.bfloat16),
            jax.ShapeDtypeStruct((32, 24, HD), jnp.float32),
        ],
        scratch_shapes=[pltpu.VMEM((384, 512), jnp.float32)],
        compiler_params=pltpu.CompilerParams(vmem_limit_bytes=24 * 2**20),
        cost_estimate=pl.CostEstimate(
            flops=2 * 384 * 512 * 256, bytes_accessed=2**20, transcendentals=0
        ),
        name="mix",
    )(info, x, w)


def ends_kernel(up_ref, down_ref, first_ref, last_ref):
    part = first_ref.shape[0]
    first_ref[...] = up_ref[:part]
    last_ref[...] = down_ref[part:]


def join_kernel(*refs):
    size = refs[0].shape[0]
    for i, ref in enumerate(refs[:-1]):
        refs[-1][i * size : (i + 1) * size] = ref[...]


def small_kernel(kernel, name, outs, args):
    vm = pl.BlockSpec(memory_space=pltpu.VMEM)
    smem = pl.BlockSpec(memory_space=pltpu.SMEM)
    return pl.pallas_call(
        kernel,
        in_specs=[smem if a.ndim == 1 else vm for a in args],
        out_specs=[vm] * len(outs),
        out_shape=[jax.ShapeDtypeStruct(o, jnp.bfloat16) for o in outs],
        compiler_params=pltpu.CompilerParams(vmem_limit_bytes=24 * 2**20),
        cost_estimate=pl.CostEstimate(flops=0, bytes_accessed=2**20, transcendentals=0),
        name=name,
    )(*args)


def project_kernel(info_ref, h_ref, *refs):
    w_refs, o_ref, h_buf, w_buf, sems = refs[:4], *refs[4:]
    x, yq = info_ref[0], info_ref[1] // 2
    copies = []
    for n in range(4):
        group = [pltpu.make_async_copy(w_refs[n], w_buf.at[n], sems.at[n, 4])]
        for back in range(4):
            block = lax.rem(x + 4 - n, 4) * 4 + lax.rem(yq + 4 - back, 4)
            group.append(
                pltpu.make_async_copy(h_ref.at[block], h_buf.at[n, back], sems.at[n, back])
            )
        copies.append(group)
        for copy in group:
            copy.start()
    total = None
    for n in range(4):
        for copy in copies[n]:
            copy.wait()
        a = jnp.concatenate([h_buf[n, i] for i in range(4)], axis=1)
        term = jnp.dot(a, w_buf[n], preferred_element_type=jnp.float32)
        total = term if total is None else total + term
    for sel in range(2):
        o_ref[sel] = total[sel * 192 : (sel + 1) * 192]


def attend_kernel(info_ref, q_ref, cos_ref, sin_ref, *refs):
    mine, other_ref, o_ref, buf, s_ref, sems = refs[:4], *refs[4:]
    rows = q_ref.shape[0]
    x, y, core = info_ref[0], info_ref[1], info_ref[2]
    size = mine[0].shape[0]

    def copies(i):
        other = other_ref.at[pl.ds(i * size, size)]
        return [
            pltpu.make_async_copy(mine[i], buf.at[i, core], sems.at[i, 0]),
            pltpu.make_async_copy(other, buf.at[i, 1 - core], sems.at[i, 1]),
        ]

    for i in range(4):

        @pl.when(x >= i)
        def _(i=i):
            for copy in copies(i):
                copy.start()

    sums = q_ref[...]
    q = sums * cos_ref[...] + pltpu.roll(sums, HD // 2, 1) * sin_ref[...]
    q = q.astype(jnp.bfloat16)

    def lanes(v, op):
        out = v[:, :HD]
        for i in range(1, v.shape[1] // HD):
            out = op(out, v[:, i * HD : (i + 1) * HD])
        return out

    def scores(k):
        return lax.dot_general(
            q, k, (((1,), (1,)), ((), ())), preferred_element_type=jnp.float32
        )

    for copy in copies(0):
        copy.wait()
    s = scores(buf[0, 0])
    qp = y * rows + lax.broadcasted_iota(jnp.int32, s.shape, 0)
    kp = lax.broadcasted_iota(jnp.int32, s.shape, 1)
    s = jnp.where(qp >= kp, s, -jnp.inf)
    s_ref[0] = s
    top = lanes(s, jnp.maximum)
    for i in range(1, 4):

        @pl.when(x >= i)
        def _(i=i):
            for copy in copies(i):
                copy.wait()

    def first_pass(i, top):
        s = scores(buf[i, 0])
        s_ref[i] = s
        return jnp.maximum(top, lanes(s, jnp.maximum))

    top = lax.fori_loop(1, x + 1, first_pass, top)
    top = jnp.max(top, axis=1, keepdims=True)
    scale = HD**-0.5 * math.log2(math.e)

    def second_pass(i, state):
        tot, acc = state
        e = jnp.exp2((s_ref[i] - top) * scale)
        return tot + lanes(e, jnp.add), acc + jnp.dot(
            e.astype(jnp.bfloat16), buf[i, 1], preferred_element_type=jnp.float32
        )

    zero = jnp.zeros((rows, HD), jnp.float32)
    tot, acc = lax.fori_loop(0, x + 1, second_pass, (zero, zero))
    o_ref[...] = (acc / jnp.sum(tot, axis=1, keepdims=True)).astype(o_ref.dtype)


def project(info, h, pieces):
    count, m, part = h.shape
    hbm = pl.BlockSpec(memory_space=pl.ANY)
    return pl.pallas_call(
        project_kernel,
        in_specs=[pl.BlockSpec(memory_space=pltpu.SMEM)] + [hbm] * 5,
        out_specs=pl.BlockSpec(memory_space=pltpu.VMEM),
        out_shape=jax.ShapeDtypeStruct((2, m // 2, HD), jnp.float32),
        scratch_shapes=[
            pltpu.VMEM((4, count // 4, m, part), jnp.bfloat16),
            pltpu.VMEM((4, count // 4 * part, HD), jnp.bfloat16),
            pltpu.SemaphoreType.DMA((4, 5)),
        ],
        compiler_params=pltpu.CompilerParams(vmem_limit_bytes=48 * 2**20),
        cost_estimate=pl.CostEstimate(
            flops=2 * m * count * part * HD,
            bytes_accessed=2 * count * part * (m + HD),
            transcendentals=0,
        ),
        name="project",
    )(info, h, *pieces)


def attend(info, sums, cosine, sine, mine, other):
    vm = pl.BlockSpec(memory_space=pltpu.VMEM)
    return pl.pallas_call(
        attend_kernel,
        in_specs=[pl.BlockSpec(memory_space=pltpu.SMEM), vm, vm, vm]
        + [pl.BlockSpec(memory_space=pl.ANY)] * 5,
        out_specs=vm,
        out_shape=jax.ShapeDtypeStruct(sums.shape, jnp.bfloat16),
        scratch_shapes=[
            pltpu.VMEM((4, 2, 1536, HD), jnp.bfloat16),
            pltpu.VMEM((4, 192, 1536), jnp.float32),
            pltpu.SemaphoreType.DMA((4, 2)),
        ],
        compiler_params=pltpu.CompilerParams(vmem_limit_bytes=40 * 2**20),
        cost_estimate=pl.CostEstimate(
            flops=4 * 192 * 6144 * HD,
            bytes_accessed=4 * 6144 * HD,
            transcendentals=192 * 6144,
        ),
        name="attend",
    )(info, sums, cosine, sine, *mine, other)


def shift(v, axis, by):
    n = lax.axis_size(axis)
    return lax.ppermute(v, axis, [(i, (i + by) % n) for i in range(n)])


def shift_up(v, axis, by):
    n = lax.axis_size(axis)
    return lax.ppermute(v, axis, [(i, i + by) for i in range(n - by)])


def swap(v, axis):
    return lax.ppermute(v, axis, [(0, 1), (1, 0)])


def body(hidden, query_weight, kv_weight):
    x, yq, yp, z, core = (lax.axis_index(a) for a in AXES)
    y = yq * 2 + yp
    base = (x * 8 + y) * 192
    info = jnp.stack([x, y, core])
    tie = lax.optimization_barrier

    (hs,) = small_kernel(slabs_kernel, "slabs", [(32, 12, 512)], (hidden,))
    hs, w = tie((hs, query_weight))
    hs = lax.all_to_all(hs, PAIR, 0, 0, tiled=True)

    one, three = shift(w, "yq", 1), shift(w, "yq", 3)
    two = shift(one, "yq", 1)
    hs, w, one, two, three = tie((hs, w, one, two, three))
    h, part = mix(info, hs, kv_weight)
    h = lax.all_gather(h, TP, axis=0, tiled=False)
    w = jnp.concatenate([w, one, two, three], axis=0)

    part = lax.all_to_all(part, PAIR, 0, 0, tiled=True)
    up, down = shift(w, "x", 1), shift(w, "x", -1)
    rows = jnp.sum(part, axis=0)
    cosine, sine = angles_of(base + z * 24 + jnp.arange(24, dtype=jnp.int32))
    rows = jnp.where(core == 0, rotate(rows, cosine, sine), rows).astype(jnp.bfloat16)
    rows = broadcast_gather(rows, ("yq", "yp", "z")).reshape(1536, HD)
    first, last = small_kernel(ends_kernel, "ends", [(1024, HD)] * 2, (up, down))
    cross = [shift(first, "x", 1), shift(last, "x", -1)]
    rows, cross = tie((rows, cross))
    mine = [rows] + [shift_up(rows, "x", d) for d in (1, 2, 3)]

    sums = project(info, h, (w, up, jnp.concatenate(cross, axis=0), down))
    keep = jnp.where(yp == 0, sums[0], sums[1])
    come = swap(jnp.where(yp == 0, sums[1], sums[0]), "yp")
    away, come = tie((mine[1:], come))
    (other,) = small_kernel(join_kernel, "join", [(6144, HD)], (rows, *away))
    other = swap(other, "core")
    cosine, sine = angles_of(base + jnp.arange(192, dtype=jnp.int32))
    cosine = jnp.concatenate([cosine, cosine], axis=1)
    sine = jnp.concatenate([-sine, sine], axis=1)
    return attend(info, keep + come, cosine, sine, mine, other)


def solution(mesh):
    in_specs = (P(AXES, None), P(CTX, TP), P(TP, None))
    out_specs = P(CTX, TP)
    return jax.shard_map(
        body, mesh=fine_mesh(mesh), in_specs=in_specs, out_specs=out_specs, check_vma=False
    )
```

```python
import math

import jax
import jax.numpy as jnp
from jax import lax
from jax.experimental import pallas as pl
from jax.experimental.pallas import tpu as pltpu
from jax.sharding import Mesh
from jax.sharding import PartitionSpec as P

HD = 128
CTX = ("x", "yq", "yp")
TP = ("z", "core")
PAIR = ("yp", "z", "core")
AXES = CTX + TP


def fine_mesh(mesh):
    return Mesh(mesh.devices.reshape(4, 4, 2, 8, 2), AXES)


def angles_of(positions):
    half = HD // 2
    exponent = jnp.arange(half, dtype=jnp.float32) * (2.0 / HD)
    frequency = jnp.power(jnp.float32(500000.0), -exponent)
    angles = positions.astype(jnp.float32)[:, None] * frequency[None, :]
    return jnp.cos(angles), jnp.sin(angles)


def rotate(field, cosine, sine):
    half = HD // 2
    first, second = field[:, :half], field[:, half:]
    return jnp.concatenate(
        [first * cosine - second * sine, second * cosine + first * sine], axis=1
    )


def broadcast_gather(x, axis):
    n = lax.axis_size(axis)
    return lax.all_to_all(
        jnp.broadcast_to(x[None], (n,) + x.shape), axis, 0, 0, tiled=True
    )


def slabs_kernel(h_ref, o_ref):
    for yp in range(2):
        for t in range(16):
            at = (2 * t + yp) * 512
            o_ref[yp * 16 + t] = h_ref[:, at : at + 512]


def mix_kernel(info_ref, x_ref, w_ref, rows_ref, o_ref, buf):
    yp = lax.rem(info_ref[1], 2)
    for i in range(32):
        buf[i * 12 : (i + 1) * 12, :] = x_ref[i].astype(jnp.float32)
    rows = buf[...].astype(jnp.bfloat16)
    rows_ref[...] = rows
    w = w_ref[pl.ds(pl.multiple_of(yp * 512, 512), 512), :]
    sums = jnp.dot(rows, w, preferred_element_type=jnp.float32)
    for i in range(16):
        for k in range(2):
            o_ref[2 * i + k] = sums[i * 24 : (i + 1) * 24, k * HD : (k + 1) * HD]


def mix(info, x, w):
    vm = pl.BlockSpec(memory_space=pltpu.VMEM)
    return pl.pallas_call(
        mix_kernel,
        in_specs=[pl.BlockSpec(memory_space=pltpu.SMEM), vm, vm],
        out_specs=[vm, vm],
        out_shape=[
            jax.ShapeDtypeStruct((384, 512), jnp.bfloat16),
            jax.ShapeDtypeStruct((32, 24, HD), jnp.float32),
        ],
        scratch_shapes=[pltpu.VMEM((384, 512), jnp.float32)],
        compiler_params=pltpu.CompilerParams(vmem_limit_bytes=24 * 2**20),
        cost_estimate=pl.CostEstimate(
            flops=2 * 384 * 512 * 256, bytes_accessed=2**20, transcendentals=0
        ),
        name="mix",
    )(info, x, w)


def ends_kernel(up_ref, down_ref, down2_ref, first_ref, last_ref):
    first_ref[...] = up_ref[:1024]
    last_ref[:512] = down_ref[1024:]
    last_ref[512:] = down2_ref[...]


def join_kernel(*refs):
    size = refs[0].shape[0]
    for i, ref in enumerate(refs[:-1]):
        refs[-1][i * size : (i + 1) * size] = ref[...]


def small_kernel(kernel, name, outs, args):
    vm = pl.BlockSpec(memory_space=pltpu.VMEM)
    smem = pl.BlockSpec(memory_space=pltpu.SMEM)
    return pl.pallas_call(
        kernel,
        in_specs=[smem if a.ndim == 1 else vm for a in args],
        out_specs=[vm] * len(outs),
        out_shape=[jax.ShapeDtypeStruct(o, jnp.bfloat16) for o in outs],
        compiler_params=pltpu.CompilerParams(vmem_limit_bytes=24 * 2**20),
        cost_estimate=pl.CostEstimate(flops=0, bytes_accessed=2**20, transcendentals=0),
        name=name,
    )(*args)


def project_kernel(info_ref, h_ref, *refs):
    w_refs, o_ref, h_buf, w_buf, sems = refs[:8], *refs[8:]
    x, yq = info_ref[0], info_ref[1] // 2
    copies = []
    for n in range(4):
        size = w_refs[2 * n].shape[0]
        group = [
            pltpu.make_async_copy(
                w_refs[2 * n], w_buf.at[n, pl.ds(0, size)], sems.at[n, 4]
            ),
            pltpu.make_async_copy(
                w_refs[2 * n + 1], w_buf.at[n, pl.ds(size, 2048 - size)], sems.at[n, 5]
            ),
        ]
        for i, back in enumerate((0, 1, 3, 2)):
            block = lax.rem(x + 4 - n, 4) * 4 + lax.rem(yq + 4 - back, 4)
            group.append(pltpu.make_async_copy(h_ref.at[block], h_buf.at[n, i], sems.at[n, i]))
        copies.append(group)
        for copy in group:
            copy.start()
    total = None
    for n in range(4):
        for copy in copies[n]:
            copy.wait()
        a = jnp.concatenate([h_buf[n, i] for i in range(4)], axis=1)
        term = jnp.dot(a, w_buf[n], preferred_element_type=jnp.float32)
        total = term if total is None else total + term
    for sel in range(2):
        o_ref[sel] = total[sel * 192 : (sel + 1) * 192]


def attend_kernel(info_ref, q_ref, cos_ref, sin_ref, *refs):
    mine, other_ref, o_ref, buf, s_ref, sems = refs[:4], *refs[4:]
    rows = q_ref.shape[0]
    x, y, core = info_ref[0], info_ref[1], info_ref[2]
    size = mine[0].shape[0]

    def copies(i):
        other = other_ref.at[pl.ds(i * size, size)]
        return [
            pltpu.make_async_copy(mine[i], buf.at[i, core], sems.at[i, 0]),
            pltpu.make_async_copy(other, buf.at[i, 1 - core], sems.at[i, 1]),
        ]

    for i in range(4):

        @pl.when(x >= i)
        def _(i=i):
            for copy in copies(i):
                copy.start()

    sums = q_ref[...]
    q = sums * cos_ref[...] + pltpu.roll(sums, HD // 2, 1) * sin_ref[...]
    q = q.astype(jnp.bfloat16)

    def lanes(v, op):
        out = v[:, :HD]
        for i in range(1, v.shape[1] // HD):
            out = op(out, v[:, i * HD : (i + 1) * HD])
        return out

    def scores(k):
        return lax.dot_general(
            q, k, (((1,), (1,)), ((), ())), preferred_element_type=jnp.float32
        )

    for copy in copies(0):
        copy.wait()
    s = scores(buf[0, 0])
    qp = y * rows + lax.broadcasted_iota(jnp.int32, s.shape, 0)
    kp = lax.broadcasted_iota(jnp.int32, s.shape, 1)
    s = jnp.where(qp >= kp, s, -jnp.inf)
    s_ref[0] = s
    top = lanes(s, jnp.maximum)
    for i in range(1, 4):

        @pl.when(x >= i)
        def _(i=i):
            for copy in copies(i):
                copy.wait()

    def first_pass(i, top):
        s = scores(buf[i, 0])
        s_ref[i] = s
        return jnp.maximum(top, lanes(s, jnp.maximum))

    top = lax.fori_loop(1, x + 1, first_pass, top)
    top = jnp.max(top, axis=1, keepdims=True)
    scale = HD**-0.5 * math.log2(math.e)

    def second_pass(i, state):
        tot, acc = state
        e = jnp.exp2((s_ref[i] - top) * scale)
        return tot + lanes(e, jnp.add), acc + jnp.dot(
            e.astype(jnp.bfloat16), buf[i, 1], preferred_element_type=jnp.float32
        )

    zero = jnp.zeros((rows, HD), jnp.float32)
    tot, acc = lax.fori_loop(0, x + 1, second_pass, (zero, zero))
    o_ref[...] = (acc / jnp.sum(tot, axis=1, keepdims=True)).astype(o_ref.dtype)


def project(info, h, pieces):
    count, m, part = h.shape
    hbm = pl.BlockSpec(memory_space=pl.ANY)
    return pl.pallas_call(
        project_kernel,
        in_specs=[pl.BlockSpec(memory_space=pltpu.SMEM)] + [hbm] * 9,
        out_specs=pl.BlockSpec(memory_space=pltpu.VMEM),
        out_shape=jax.ShapeDtypeStruct((2, m // 2, HD), jnp.float32),
        scratch_shapes=[
            pltpu.VMEM((4, count // 4, m, part), jnp.bfloat16),
            pltpu.VMEM((4, count // 4 * part, HD), jnp.bfloat16),
            pltpu.SemaphoreType.DMA((4, 6)),
        ],
        compiler_params=pltpu.CompilerParams(vmem_limit_bytes=48 * 2**20),
        cost_estimate=pl.CostEstimate(
            flops=2 * m * count * part * HD,
            bytes_accessed=2 * count * part * (m + HD),
            transcendentals=0,
        ),
        name="project",
    )(info, h, *pieces)


def attend(info, sums, cosine, sine, mine, other):
    vm = pl.BlockSpec(memory_space=pltpu.VMEM)
    return pl.pallas_call(
        attend_kernel,
        in_specs=[pl.BlockSpec(memory_space=pltpu.SMEM), vm, vm, vm]
        + [pl.BlockSpec(memory_space=pl.ANY)] * 5,
        out_specs=vm,
        out_shape=jax.ShapeDtypeStruct(sums.shape, jnp.bfloat16),
        scratch_shapes=[
            pltpu.VMEM((4, 2, 1536, HD), jnp.bfloat16),
            pltpu.VMEM((4, 192, 1536), jnp.float32),
            pltpu.SemaphoreType.DMA((4, 2)),
        ],
        compiler_params=pltpu.CompilerParams(vmem_limit_bytes=40 * 2**20),
        cost_estimate=pl.CostEstimate(
            flops=4 * 192 * 6144 * HD,
            bytes_accessed=4 * 6144 * HD,
            transcendentals=192 * 6144,
        ),
        name="attend",
    )(info, sums, cosine, sine, *mine, other)


def shift(v, axis, by):
    n = lax.axis_size(axis)
    return lax.ppermute(v, axis, [(i, (i + by) % n) for i in range(n)])


def shift_up(v, axis, by):
    n = lax.axis_size(axis)
    return lax.ppermute(v, axis, [(i, i + by) for i in range(n - by)])


def swap(v, axis):
    return lax.ppermute(v, axis, [(0, 1), (1, 0)])


def body(hidden, query_weight, kv_weight):
    x, yq, yp, z, core = (lax.axis_index(a) for a in AXES)
    y = yq * 2 + yp
    base = (x * 8 + y) * 192
    info = jnp.stack([x, y, core])
    tie = lax.optimization_barrier

    (hs,) = small_kernel(slabs_kernel, "slabs", [(32, 12, 512)], (hidden,))
    hs, w = tie((hs, query_weight))
    hs = lax.all_to_all(hs, PAIR, 0, 0, tiled=True)

    one, three = shift(w, "yq", 1), shift(w, "yq", 3)
    hs, w, one, three = tie((hs, w, one, three))
    h, part = mix(info, hs, kv_weight)
    h = lax.all_gather(h, TP, axis=0, tiled=False)
    two = shift(one, "yq", 1)
    w = jnp.concatenate([w, one, three], axis=0)

    part = lax.all_to_all(part, PAIR, 0, 0, tiled=True)
    up, down = shift(w, "x", 1), shift(w, "x", -1)
    rows = jnp.sum(part, axis=0)
    cosine, sine = angles_of(base + z * 24 + jnp.arange(24, dtype=jnp.int32))
    rows = jnp.where(core == 0, rotate(rows, cosine, sine), rows).astype(jnp.bfloat16)
    rows = broadcast_gather(rows, ("yq", "yp", "z")).reshape(1536, HD)
    up2, down2 = shift(two, "x", 1), shift(two, "x", -1)
    rows, up, down, up2, down2 = tie((rows, up, down, up2, down2))
    first, last = small_kernel(ends_kernel, "ends", [(1024, HD)] * 2, (up, down, down2))
    cross = [shift(first, "x", 1), shift(last, "x", -1)]
    mine = [rows] + [shift_up(rows, "x", d) for d in (1, 2, 3)]

    sums = project(info, h, (w, two, up, up2, *cross, down, down2))
    keep = jnp.where(yp == 0, sums[0], sums[1])
    come = swap(jnp.where(yp == 0, sums[1], sums[0]), "yp")
    away, come = tie((mine[1:], come))
    (other,) = small_kernel(join_kernel, "join", [(6144, HD)], (rows, *away))
    other = swap(other, "core")
    cosine, sine = angles_of(base + jnp.arange(192, dtype=jnp.int32))
    cosine = jnp.concatenate([cosine, cosine], axis=1)
    sine = jnp.concatenate([-sine, sine], axis=1)
    return attend(info, keep + come, cosine, sine, mine, other)


def solution(mesh):
    in_specs = (P(AXES, None), P(CTX, TP), P(TP, None))
    out_specs = P(CTX, TP)
    return jax.shard_map(
        body, mesh=fine_mesh(mesh), in_specs=in_specs, out_specs=out_specs, check_vma=False
    )
```

```python
import math

import jax
import jax.numpy as jnp
from jax import lax
from jax.experimental import pallas as pl
from jax.experimental.pallas import tpu as pltpu
from jax.sharding import Mesh
from jax.sharding import PartitionSpec as P

HD = 128
CTX = ("x", "yq", "yp")
TP = ("z", "core")
PAIR = ("yp", "z", "core")
AXES = CTX + TP


def fine_mesh(mesh):
    return Mesh(mesh.devices.reshape(4, 4, 2, 8, 2), AXES)


def angles_of(positions):
    half = HD // 2
    exponent = jnp.arange(half, dtype=jnp.float32) * (2.0 / HD)
    frequency = jnp.power(jnp.float32(500000.0), -exponent)
    angles = positions.astype(jnp.float32)[:, None] * frequency[None, :]
    return jnp.cos(angles), jnp.sin(angles)


def rotate(field, cosine, sine):
    half = HD // 2
    first, second = field[:, :half], field[:, half:]
    return jnp.concatenate(
        [first * cosine - second * sine, second * cosine + first * sine], axis=1
    )


def broadcast_gather(x, axis):
    n = lax.axis_size(axis)
    return lax.all_to_all(
        jnp.broadcast_to(x[None], (n,) + x.shape), axis, 0, 0, tiled=True
    )


def slabs_kernel(h_ref, o_ref):
    for yp in range(2):
        for t in range(16):
            at = (2 * t + yp) * 512
            o_ref[yp * 16 + t] = h_ref[:, at : at + 512]


def mix_kernel(info_ref, x_ref, w_ref, rows_ref, o_ref, buf):
    yp = lax.rem(info_ref[1], 2)
    for i in range(32):
        buf[i * 12 : (i + 1) * 12, :] = x_ref[i].astype(jnp.float32)
    rows = buf[...].astype(jnp.bfloat16)
    rows_ref[...] = rows
    w = w_ref[pl.ds(pl.multiple_of(yp * 512, 512), 512), :]
    sums = jnp.dot(rows, w, preferred_element_type=jnp.float32)
    for i in range(16):
        for k in range(2):
            o_ref[2 * i + k] = sums[i * 24 : (i + 1) * 24, k * HD : (k + 1) * HD]


def mix(info, x, w):
    vm = pl.BlockSpec(memory_space=pltpu.VMEM)
    return pl.pallas_call(
        mix_kernel,
        in_specs=[pl.BlockSpec(memory_space=pltpu.SMEM), vm, vm],
        out_specs=[vm, vm],
        out_shape=[
            jax.ShapeDtypeStruct((384, 512), jnp.bfloat16),
            jax.ShapeDtypeStruct((32, 24, HD), jnp.float32),
        ],
        scratch_shapes=[pltpu.VMEM((384, 512), jnp.float32)],
        compiler_params=pltpu.CompilerParams(vmem_limit_bytes=24 * 2**20),
        cost_estimate=pl.CostEstimate(
            flops=2 * 384 * 512 * 256, bytes_accessed=2**20, transcendentals=0
        ),
        name="mix",
    )(info, x, w)


def ends_kernel(up_ref, down_ref, first_ref, last_ref):
    part = first_ref.shape[0]
    first_ref[...] = up_ref[:part]
    last_ref[...] = down_ref[part:]


def join_kernel(*refs):
    size = refs[0].shape[0]
    for i, ref in enumerate(refs[:-1]):
        refs[-1][i * size : (i + 1) * size] = ref[...]


def small_kernel(kernel, name, outs, args):
    vm = pl.BlockSpec(memory_space=pltpu.VMEM)
    smem = pl.BlockSpec(memory_space=pltpu.SMEM)
    return pl.pallas_call(
        kernel,
        in_specs=[smem if a.ndim == 1 else vm for a in args],
        out_specs=[vm] * len(outs),
        out_shape=[jax.ShapeDtypeStruct(o, jnp.bfloat16) for o in outs],
        compiler_params=pltpu.CompilerParams(vmem_limit_bytes=24 * 2**20),
        cost_estimate=pl.CostEstimate(flops=0, bytes_accessed=2**20, transcendentals=0),
        name=name,
    )(*args)


def project_kernel(info_ref, h_ref, *refs):
    w_refs, o_ref, h_buf, w_buf, sems = refs[:4], *refs[4:]
    x, yq = info_ref[0], info_ref[1] // 2
    copies = []
    for n in range(4):
        group = [pltpu.make_async_copy(w_refs[n], w_buf.at[n], sems.at[n, 4])]
        for back in range(4):
            block = lax.rem(x + 4 - n, 4) * 4 + lax.rem(yq + 4 - back, 4)
            group.append(
                pltpu.make_async_copy(h_ref.at[block], h_buf.at[n, back], sems.at[n, back])
            )
        copies.append(group)
        for copy in group:
            copy.start()
    total = None
    for n in range(4):
        for copy in copies[n]:
            copy.wait()
        a = jnp.concatenate([h_buf[n, i] for i in range(4)], axis=1)
        term = jnp.dot(a, w_buf[n], preferred_element_type=jnp.float32)
        total = term if total is None else total + term
    for sel in range(2):
        o_ref[sel] = total[sel * 192 : (sel + 1) * 192]


def attend_kernel(info_ref, q_ref, cos_ref, sin_ref, *refs):
    mine, other_ref, o_ref, buf, s_ref, sems = refs[:4], *refs[4:]
    rows = q_ref.shape[0]
    x, y, core = info_ref[0], info_ref[1], info_ref[2]
    size = mine[0].shape[0]

    def copies(i):
        other = other_ref.at[pl.ds(i * size, size)]
        return [
            pltpu.make_async_copy(mine[i], buf.at[i, core], sems.at[i, 0]),
            pltpu.make_async_copy(other, buf.at[i, 1 - core], sems.at[i, 1]),
        ]

    for values in range(2):
        for i in range(4):
            for own in range(2):

                @pl.when((x >= i) & (core == own))
                def _(i=i, which=(own + values) % 2):
                    copies(i)[which].start()

    def wait(i, values):
        which = jnp.where(core == 0, values, 1 - values)
        pltpu.make_async_copy(mine[0], buf.at[i, values], sems.at[i, which]).wait()

    sums = q_ref[...]
    q = sums * cos_ref[...] + pltpu.roll(sums, HD // 2, 1) * sin_ref[...]
    q = q.astype(jnp.bfloat16)

    def lanes(v, op):
        out = v[:, :HD]
        for i in range(1, v.shape[1] // HD):
            out = op(out, v[:, i * HD : (i + 1) * HD])
        return out

    def scores(k):
        return lax.dot_general(
            q, k, (((1,), (1,)), ((), ())), preferred_element_type=jnp.float32
        )

    wait(0, 0)
    s = scores(buf[0, 0])
    qp = y * rows + lax.broadcasted_iota(jnp.int32, s.shape, 0)
    kp = lax.broadcasted_iota(jnp.int32, s.shape, 1)
    s = jnp.where(qp >= kp, s, -jnp.inf)
    s_ref[0] = s
    top = lanes(s, jnp.maximum)

    def first_pass(i, top):
        wait(i, 0)
        s = scores(buf[i, 0])
        s_ref[i] = s
        return jnp.maximum(top, lanes(s, jnp.maximum))

    top = lax.fori_loop(1, x + 1, first_pass, top)
    top = jnp.max(top, axis=1, keepdims=True)
    scale = HD**-0.5 * math.log2(math.e)

    def second_pass(i, state):
        tot, acc = state
        wait(i, 1)
        e = jnp.exp2((s_ref[i] - top) * scale)
        return tot + lanes(e, jnp.add), acc + jnp.dot(
            e.astype(jnp.bfloat16), buf[i, 1], preferred_element_type=jnp.float32
        )

    zero = jnp.zeros((rows, HD), jnp.float32)
    tot, acc = lax.fori_loop(0, x + 1, second_pass, (zero, zero))
    o_ref[...] = (acc / jnp.sum(tot, axis=1, keepdims=True)).astype(o_ref.dtype)


def project(info, h, pieces):
    count, m, part = h.shape
    hbm = pl.BlockSpec(memory_space=pl.ANY)
    return pl.pallas_call(
        project_kernel,
        in_specs=[pl.BlockSpec(memory_space=pltpu.SMEM)] + [hbm] * 5,
        out_specs=pl.BlockSpec(memory_space=pltpu.VMEM),
        out_shape=jax.ShapeDtypeStruct((2, m // 2, HD), jnp.float32),
        scratch_shapes=[
            pltpu.VMEM((4, count // 4, m, part), jnp.bfloat16),
            pltpu.VMEM((4, count // 4 * part, HD), jnp.bfloat16),
            pltpu.SemaphoreType.DMA((4, 5)),
        ],
        compiler_params=pltpu.CompilerParams(vmem_limit_bytes=48 * 2**20),
        cost_estimate=pl.CostEstimate(
            flops=2 * m * count * part * HD,
            bytes_accessed=2 * count * part * (m + HD),
            transcendentals=0,
        ),
        name="project",
    )(info, h, *pieces)


def attend(info, sums, cosine, sine, mine, other):
    vm = pl.BlockSpec(memory_space=pltpu.VMEM)
    return pl.pallas_call(
        attend_kernel,
        in_specs=[pl.BlockSpec(memory_space=pltpu.SMEM), vm, vm, vm]
        + [pl.BlockSpec(memory_space=pl.ANY)] * 5,
        out_specs=vm,
        out_shape=jax.ShapeDtypeStruct(sums.shape, jnp.bfloat16),
        scratch_shapes=[
            pltpu.VMEM((4, 2, 1536, HD), jnp.bfloat16),
            pltpu.VMEM((4, 192, 1536), jnp.float32),
            pltpu.SemaphoreType.DMA((4, 2)),
        ],
        compiler_params=pltpu.CompilerParams(vmem_limit_bytes=40 * 2**20),
        cost_estimate=pl.CostEstimate(
            flops=4 * 192 * 6144 * HD,
            bytes_accessed=4 * 6144 * HD,
            transcendentals=192 * 6144,
        ),
        name="attend",
    )(info, sums, cosine, sine, *mine, other)


def shift(v, axis, by):
    n = lax.axis_size(axis)
    return lax.ppermute(v, axis, [(i, (i + by) % n) for i in range(n)])


def shift_up(v, axis, by):
    n = lax.axis_size(axis)
    return lax.ppermute(v, axis, [(i, i + by) for i in range(n - by)])


def swap(v, axis):
    return lax.ppermute(v, axis, [(0, 1), (1, 0)])


def body(hidden, query_weight, kv_weight):
    x, yq, yp, z, core = (lax.axis_index(a) for a in AXES)
    y = yq * 2 + yp
    base = (x * 8 + y) * 192
    info = jnp.stack([x, y, core])
    tie = lax.optimization_barrier

    (hs,) = small_kernel(slabs_kernel, "slabs", [(32, 12, 512)], (hidden,))
    hs, w = tie((hs, query_weight))
    hs = lax.all_to_all(hs, PAIR, 0, 0, tiled=True)

    one, three = shift(w, "yq", 1), shift(w, "yq", 3)
    hs, w, one, three = tie((hs, w, one, three))
    h, part = mix(info, hs, kv_weight)
    h = lax.all_gather(h, TP, axis=0, tiled=False)
    w = jnp.concatenate([w, one, shift(one, "yq", 1), three], axis=0)

    part = lax.all_to_all(part, PAIR, 0, 0, tiled=True)
    up, down = shift(w, "x", 1), shift(w, "x", -1)
    rows = jnp.sum(part, axis=0)
    cosine, sine = angles_of(base + z * 24 + jnp.arange(24, dtype=jnp.int32))
    rows = jnp.where(core == 0, rotate(rows, cosine, sine), rows).astype(jnp.bfloat16)
    rows = broadcast_gather(rows, ("yq", "yp", "z")).reshape(1536, HD)
    first, last = small_kernel(ends_kernel, "ends", [(1024, HD)] * 2, (up, down))
    cross = [shift(first, "x", 1), shift(last, "x", -1)]
    rows, cross = tie((rows, cross))
    mine = [rows] + [shift_up(rows, "x", d) for d in (1, 2, 3)]

    sums = project(info, h, (w, up, jnp.concatenate(cross, axis=0), down))
    keep = jnp.where(yp == 0, sums[0], sums[1])
    come = swap(jnp.where(yp == 0, sums[1], sums[0]), "yp")
    away, come = tie((mine[1:], come))
    (other,) = small_kernel(join_kernel, "join", [(6144, HD)], (rows, *away))
    other = swap(other, "core")
    cosine, sine = angles_of(base + jnp.arange(192, dtype=jnp.int32))
    cosine = jnp.concatenate([cosine, cosine], axis=1)
    sine = jnp.concatenate([-sine, sine], axis=1)
    return attend(info, keep + come, cosine, sine, mine, other)


def solution(mesh):
    in_specs = (P(AXES, None), P(CTX, TP), P(TP, None))
    out_specs = P(CTX, TP)
    return jax.shard_map(
        body, mesh=fine_mesh(mesh), in_specs=in_specs, out_specs=out_specs, check_vma=False
    )
```

```python
import math

import jax
import jax.numpy as jnp
from jax import lax
from jax.experimental import pallas as pl
from jax.experimental.pallas import tpu as pltpu
from jax.sharding import Mesh
from jax.sharding import PartitionSpec as P

HD = 128
CTX = ("x", "yq", "yp")
TP = ("z", "core")
PAIR = ("yp", "z", "core")
AXES = CTX + TP


def fine_mesh(mesh):
    return Mesh(mesh.devices.reshape(4, 4, 2, 8, 2), AXES)


def angles_of(positions):
    half = HD // 2
    exponent = jnp.arange(half, dtype=jnp.float32) * (2.0 / HD)
    frequency = jnp.power(jnp.float32(500000.0), -exponent)
    angles = positions.astype(jnp.float32)[:, None] * frequency[None, :]
    return jnp.cos(angles), jnp.sin(angles)


def rotate(field, cosine, sine):
    half = HD // 2
    first, second = field[:, :half], field[:, half:]
    return jnp.concatenate(
        [first * cosine - second * sine, second * cosine + first * sine], axis=1
    )


def broadcast_gather(x, axis):
    n = lax.axis_size(axis)
    return lax.all_to_all(
        jnp.broadcast_to(x[None], (n,) + x.shape), axis, 0, 0, tiled=True
    )


def slabs_kernel(h_ref, o_ref):
    for yp in range(2):
        for t in range(16):
            at = (2 * t + yp) * 512
            o_ref[yp * 16 + t] = h_ref[:, at : at + 512]


def mix_kernel(info_ref, x_ref, w_ref, rows_ref, o_ref, buf):
    yp = lax.rem(info_ref[1], 2)
    for i in range(32):
        buf[i * 12 : (i + 1) * 12, :] = x_ref[i].astype(jnp.float32)
    rows = buf[...].astype(jnp.bfloat16)
    rows_ref[...] = rows
    w = w_ref[pl.ds(pl.multiple_of(yp * 512, 512), 512), :]
    sums = jnp.dot(rows, w, preferred_element_type=jnp.float32)
    for i in range(16):
        for k in range(2):
            o_ref[2 * i + k] = sums[i * 24 : (i + 1) * 24, k * HD : (k + 1) * HD]


def mix(info, x, w):
    vm = pl.BlockSpec(memory_space=pltpu.VMEM)
    return pl.pallas_call(
        mix_kernel,
        in_specs=[pl.BlockSpec(memory_space=pltpu.SMEM), vm, vm],
        out_specs=[vm, vm],
        out_shape=[
            jax.ShapeDtypeStruct((384, 512), jnp.bfloat16),
            jax.ShapeDtypeStruct((32, 24, HD), jnp.float32),
        ],
        scratch_shapes=[pltpu.VMEM((384, 512), jnp.float32)],
        compiler_params=pltpu.CompilerParams(vmem_limit_bytes=24 * 2**20),
        cost_estimate=pl.CostEstimate(
            flops=2 * 384 * 512 * 256, bytes_accessed=2**20, transcendentals=0
        ),
        name="mix",
    )(info, x, w)


def ends_kernel(up_ref, down_ref, first_ref, last_ref):
    part = first_ref.shape[0]
    first_ref[...] = up_ref[:part]
    last_ref[...] = down_ref[part:]


def join_kernel(*refs):
    size = refs[0].shape[0]
    for i, ref in enumerate(refs[:-1]):
        refs[-1][i * size : (i + 1) * size] = ref[...]


def small_kernel(kernel, name, outs, args):
    vm = pl.BlockSpec(memory_space=pltpu.VMEM)
    smem = pl.BlockSpec(memory_space=pltpu.SMEM)
    return pl.pallas_call(
        kernel,
        in_specs=[smem if a.ndim == 1 else vm for a in args],
        out_specs=[vm] * len(outs),
        out_shape=[jax.ShapeDtypeStruct(o, jnp.bfloat16) for o in outs],
        compiler_params=pltpu.CompilerParams(vmem_limit_bytes=24 * 2**20),
        cost_estimate=pl.CostEstimate(flops=0, bytes_accessed=2**20, transcendentals=0),
        name=name,
    )(*args)


def project_kernel(info_ref, h_ref, *refs):
    w_refs, o_ref, h_buf, w_buf, sems = refs[:4], *refs[4:]
    x, yq = info_ref[0], info_ref[1] // 2
    copies = []
    for n in range(4):
        group = [pltpu.make_async_copy(w_refs[n], w_buf.at[n], sems.at[n, 4])]
        for back in range(4):
            block = lax.rem(x + 4 - n, 4) * 4 + lax.rem(yq + 4 - back, 4)
            group.append(
                pltpu.make_async_copy(h_ref.at[block], h_buf.at[n, back], sems.at[n, back])
            )
        copies.append(group)
        for copy in group:
            copy.start()
    total = None
    for n in range(4):
        for copy in copies[n]:
            copy.wait()
        a = jnp.concatenate([h_buf[n, i] for i in range(4)], axis=1)
        term = jnp.dot(a, w_buf[n], preferred_element_type=jnp.float32)
        total = term if total is None else total + term
    for sel in range(2):
        o_ref[sel] = total[sel * 192 : (sel + 1) * 192]


def attend_kernel(info_ref, q_ref, cos_ref, sin_ref, *refs):
    mine, other_ref, o_ref, buf, s_ref, sems = refs[:4], *refs[4:]
    rows = q_ref.shape[0]
    x, y, core = info_ref[0], info_ref[1], info_ref[2]
    size = mine[0].shape[0]

    def copies(i):
        other = other_ref.at[pl.ds(i * size, size)]
        return [
            pltpu.make_async_copy(mine[i], buf.at[i, core], sems.at[i, 0]),
            pltpu.make_async_copy(other, buf.at[i, 1 - core], sems.at[i, 1]),
        ]

    for i in range(4):

        @pl.when(x >= i)
        def _(i=i):
            for copy in copies(i):
                copy.start()

    sums = q_ref[...]
    q = sums * cos_ref[...] + pltpu.roll(sums, HD // 2, 1) * sin_ref[...]
    q = q.astype(jnp.bfloat16)

    def lanes(v, op):
        out = v[:, :HD]
        for i in range(1, v.shape[1] // HD):
            out = op(out, v[:, i * HD : (i + 1) * HD])
        return out

    def scores(k):
        return lax.dot_general(
            q, k, (((1,), (1,)), ((), ())), preferred_element_type=jnp.float32
        )

    for copy in copies(0):
        copy.wait()
    s = scores(buf[0, 0])
    qp = y * rows + lax.broadcasted_iota(jnp.int32, s.shape, 0)
    kp = lax.broadcasted_iota(jnp.int32, s.shape, 1)
    s = jnp.where(qp >= kp, s, -jnp.inf)
    s_ref[0] = s
    top = lanes(s, jnp.maximum)
    for i in range(1, 4):

        @pl.when(x >= i)
        def _(i=i):
            for copy in copies(i):
                copy.wait()

    def first_pass(i, top):
        s = scores(buf[i, 0])
        s_ref[i] = s
        return jnp.maximum(top, lanes(s, jnp.maximum))

    top = lax.fori_loop(1, x + 1, first_pass, top)
    top = jnp.max(top, axis=1, keepdims=True)
    scale = HD**-0.5 * math.log2(math.e)

    def second_pass(i, state):
        tot, acc = state
        e = jnp.exp2((s_ref[i] - top) * scale)
        return tot + lanes(e, jnp.add), acc + jnp.dot(
            e.astype(jnp.bfloat16), buf[i, 1], preferred_element_type=jnp.float32
        )

    zero = jnp.zeros((rows, HD), jnp.float32)
    tot, acc = lax.fori_loop(0, x + 1, second_pass, (zero, zero))
    o_ref[...] = (acc / jnp.sum(tot, axis=1, keepdims=True)).astype(o_ref.dtype)


def project(info, h, pieces):
    count, m, part = h.shape
    hbm = pl.BlockSpec(memory_space=pl.ANY)
    return pl.pallas_call(
        project_kernel,
        in_specs=[pl.BlockSpec(memory_space=pltpu.SMEM)] + [hbm] * 5,
        out_specs=pl.BlockSpec(memory_space=pltpu.VMEM),
        out_shape=jax.ShapeDtypeStruct((2, m // 2, HD), jnp.float32),
        scratch_shapes=[
            pltpu.VMEM((4, count // 4, m, part), jnp.bfloat16),
            pltpu.VMEM((4, count // 4 * part, HD), jnp.bfloat16),
            pltpu.SemaphoreType.DMA((4, 5)),
        ],
        compiler_params=pltpu.CompilerParams(vmem_limit_bytes=48 * 2**20),
        cost_estimate=pl.CostEstimate(
            flops=2 * m * count * part * HD,
            bytes_accessed=2 * count * part * (m + HD),
            transcendentals=0,
        ),
        name="project",
    )(info, h, *pieces)


def attend(info, sums, cosine, sine, mine, other):
    vm = pl.BlockSpec(memory_space=pltpu.VMEM)
    return pl.pallas_call(
        attend_kernel,
        in_specs=[pl.BlockSpec(memory_space=pltpu.SMEM), vm, vm, vm]
        + [pl.BlockSpec(memory_space=pl.ANY)] * 5,
        out_specs=vm,
        out_shape=jax.ShapeDtypeStruct(sums.shape, jnp.bfloat16),
        scratch_shapes=[
            pltpu.VMEM((4, 2, 1536, HD), jnp.bfloat16),
            pltpu.VMEM((4, 192, 1536), jnp.float32),
            pltpu.SemaphoreType.DMA((4, 2)),
        ],
        compiler_params=pltpu.CompilerParams(vmem_limit_bytes=40 * 2**20),
        cost_estimate=pl.CostEstimate(
            flops=4 * 192 * 6144 * HD,
            bytes_accessed=4 * 6144 * HD,
            transcendentals=192 * 6144,
        ),
        name="attend",
    )(info, sums, cosine, sine, *mine, other)


def shift(v, axis, by):
    n = lax.axis_size(axis)
    return lax.ppermute(v, axis, [(i, (i + by) % n) for i in range(n)])


def shift_up(v, axis, by):
    n = lax.axis_size(axis)
    return lax.ppermute(v, axis, [(i, i + by) for i in range(n - by)])


def swap(v, axis):
    return lax.ppermute(v, axis, [(0, 1), (1, 0)])


def body(hidden, query_weight, kv_weight):
    x, yq, yp, z, core = (lax.axis_index(a) for a in AXES)
    y = yq * 2 + yp
    base = (x * 8 + y) * 192
    info = jnp.stack([x, y, core])
    tie = lax.optimization_barrier

    (hs,) = small_kernel(slabs_kernel, "slabs", [(32, 12, 512)], (hidden,))
    hs, w = tie((hs, query_weight))
    hs = lax.all_to_all(hs, PAIR, 0, 0, tiled=True)

    one, three = shift(w, "yq", 1), shift(w, "yq", 3)
    hs, w, one, three = tie((hs, w, one, three))
    h, part = mix(info, hs, kv_weight)
    h = lax.all_gather(h, TP, axis=0, tiled=False)
    two = shift(one, "yq", 1)
    part, two = tie((part, two))
    w = jnp.concatenate([w, one, two, three], axis=0)

    part = lax.all_to_all(part, PAIR, 0, 0, tiled=True)
    up, down = shift(w, "x", 1), shift(w, "x", -1)
    rows = jnp.sum(part, axis=0)
    cosine, sine = angles_of(base + z * 24 + jnp.arange(24, dtype=jnp.int32))
    rows = jnp.where(core == 0, rotate(rows, cosine, sine), rows).astype(jnp.bfloat16)
    rows = broadcast_gather(rows, ("yq", "yp", "z")).reshape(1536, HD)
    first, last = small_kernel(ends_kernel, "ends", [(1024, HD)] * 2, (up, down))
    cross = [shift(first, "x", 1), shift(last, "x", -1)]
    rows, cross = tie((rows, cross))
    mine = [rows] + [shift_up(rows, "x", d) for d in (1, 2, 3)]

    sums = project(info, h, (w, up, jnp.concatenate(cross, axis=0), down))
    keep = jnp.where(yp == 0, sums[0], sums[1])
    come = swap(jnp.where(yp == 0, sums[1], sums[0]), "yp")
    away, come = tie((mine[1:], come))
    (other,) = small_kernel(join_kernel, "join", [(6144, HD)], (rows, *away))
    other = swap(other, "core")
    cosine, sine = angles_of(base + jnp.arange(192, dtype=jnp.int32))
    cosine = jnp.concatenate([cosine, cosine], axis=1)
    sine = jnp.concatenate([-sine, sine], axis=1)
    return attend(info, keep + come, cosine, sine, mine, other)


def solution(mesh):
    in_specs = (P(AXES, None), P(CTX, TP), P(TP, None))
    out_specs = P(CTX, TP)
    return jax.shard_map(
        body, mesh=fine_mesh(mesh), in_specs=in_specs, out_specs=out_specs, check_vma=False
    )
```

```python
import math

import jax
import jax.numpy as jnp
from jax import lax
from jax.experimental import pallas as pl
from jax.experimental.pallas import tpu as pltpu
from jax.sharding import Mesh
from jax.sharding import PartitionSpec as P

HD = 128
CTX = ("x", "yq", "yp")
TP = ("z", "core")
PAIR = ("yp", "z", "core")
AXES = CTX + TP


def fine_mesh(mesh):
    return Mesh(mesh.devices.reshape(4, 4, 2, 8, 2), AXES)


def angles_of(positions):
    half = HD // 2
    exponent = jnp.arange(half, dtype=jnp.float32) * (2.0 / HD)
    frequency = jnp.power(jnp.float32(500000.0), -exponent)
    angles = positions.astype(jnp.float32)[:, None] * frequency[None, :]
    return jnp.cos(angles), jnp.sin(angles)


def rotate(field, cosine, sine):
    half = HD // 2
    first, second = field[:, :half], field[:, half:]
    return jnp.concatenate(
        [first * cosine - second * sine, second * cosine + first * sine], axis=1
    )


def broadcast_gather(x, axis):
    n = lax.axis_size(axis)
    return lax.all_to_all(
        jnp.broadcast_to(x[None], (n,) + x.shape), axis, 0, 0, tiled=True
    )


def slabs_kernel(h_ref, o_ref):
    for yp in range(2):
        for t in range(16):
            at = (2 * t + yp) * 512
            o_ref[yp * 16 + t] = h_ref[:, at : at + 512]


def mix_kernel(info_ref, x_ref, w_ref, rows_ref, o_ref, buf):
    yp = lax.rem(info_ref[1], 2)
    for i in range(32):
        buf[i * 12 : (i + 1) * 12, :] = x_ref[i].astype(jnp.float32)
    rows = buf[...].astype(jnp.bfloat16)
    rows_ref[...] = rows
    w = w_ref[pl.ds(pl.multiple_of(yp * 512, 512), 512), :]
    sums = jnp.dot(rows, w, preferred_element_type=jnp.float32)
    for i in range(16):
        for k in range(2):
            o_ref[2 * i + k] = sums[i * 24 : (i + 1) * 24, k * HD : (k + 1) * HD]


def mix(info, x, w):
    vm = pl.BlockSpec(memory_space=pltpu.VMEM)
    return pl.pallas_call(
        mix_kernel,
        in_specs=[pl.BlockSpec(memory_space=pltpu.SMEM), vm, vm],
        out_specs=[vm, vm],
        out_shape=[
            jax.ShapeDtypeStruct((384, 512), jnp.bfloat16),
            jax.ShapeDtypeStruct((32, 24, HD), jnp.float32),
        ],
        scratch_shapes=[pltpu.VMEM((384, 512), jnp.float32)],
        compiler_params=pltpu.CompilerParams(vmem_limit_bytes=24 * 2**20),
        cost_estimate=pl.CostEstimate(
            flops=2 * 384 * 512 * 256, bytes_accessed=2**20, transcendentals=0
        ),
        name="mix",
    )(info, x, w)


def ends_kernel(up_ref, down_ref, first_ref, last_ref):
    part = first_ref.shape[0]
    first_ref[...] = up_ref[:part]
    last_ref[...] = down_ref[part:]


def join_kernel(*refs):
    size = refs[0].shape[0]
    for i, ref in enumerate(refs[:-1]):
        refs[-1][i * size : (i + 1) * size] = ref[...]


def small_kernel(kernel, name, outs, args):
    vm = pl.BlockSpec(memory_space=pltpu.VMEM)
    smem = pl.BlockSpec(memory_space=pltpu.SMEM)
    return pl.pallas_call(
        kernel,
        in_specs=[smem if a.ndim == 1 else vm for a in args],
        out_specs=[vm] * len(outs),
        out_shape=[jax.ShapeDtypeStruct(o, jnp.bfloat16) for o in outs],
        compiler_params=pltpu.CompilerParams(vmem_limit_bytes=24 * 2**20),
        cost_estimate=pl.CostEstimate(flops=0, bytes_accessed=2**20, transcendentals=0),
        name=name,
    )(*args)


def project_kernel(info_ref, h_ref, *refs):
    w_refs, o_ref, h_buf, w_buf, sems = refs[:4], *refs[4:]
    x, yq = info_ref[0], info_ref[1] // 2
    copies = []
    for n in range(4):
        group = [pltpu.make_async_copy(w_refs[n], w_buf.at[n], sems.at[n, 4])]
        for back in range(4):
            block = lax.rem(x + 4 - n, 4) * 4 + lax.rem(yq + 4 - back, 4)
            group.append(
                pltpu.make_async_copy(h_ref.at[block], h_buf.at[n, back], sems.at[n, back])
            )
        copies.append(group)
        for copy in group:
            copy.start()
    total = None
    for n in range(4):
        for copy in copies[n]:
            copy.wait()
        a = jnp.concatenate([h_buf[n, i] for i in range(4)], axis=1)
        term = jnp.dot(a, w_buf[n], preferred_element_type=jnp.float32)
        total = term if total is None else total + term
    for sel in range(2):
        o_ref[sel] = total[sel * 192 : (sel + 1) * 192]


def attend_kernel(info_ref, q_ref, cos_ref, sin_ref, *refs):
    mine, near_ref, far_ref, o_ref, buf, s_ref, sems = refs[:4], *refs[4:]
    rows = q_ref.shape[0]
    x, y, core = info_ref[0], info_ref[1], info_ref[2]
    size = mine[0].shape[0]

    def copies(i):
        other = near_ref if i == 0 else far_ref.at[pl.ds((i - 1) * size, size)]
        return [
            pltpu.make_async_copy(mine[i], buf.at[i, core], sems.at[i, 0]),
            pltpu.make_async_copy(other, buf.at[i, 1 - core], sems.at[i, 1]),
        ]

    for i in range(4):

        @pl.when(x >= i)
        def _(i=i):
            for copy in copies(i):
                copy.start()

    sums = q_ref[...]
    q = sums * cos_ref[...] + pltpu.roll(sums, HD // 2, 1) * sin_ref[...]
    q = q.astype(jnp.bfloat16)

    def lanes(v, op):
        out = v[:, :HD]
        for i in range(1, v.shape[1] // HD):
            out = op(out, v[:, i * HD : (i + 1) * HD])
        return out

    def scores(k):
        return lax.dot_general(
            q, k, (((1,), (1,)), ((), ())), preferred_element_type=jnp.float32
        )

    for copy in copies(0):
        copy.wait()
    s = scores(buf[0, 0])
    qp = y * rows + lax.broadcasted_iota(jnp.int32, s.shape, 0)
    kp = lax.broadcasted_iota(jnp.int32, s.shape, 1)
    s = jnp.where(qp >= kp, s, -jnp.inf)
    s_ref[0] = s
    top = lanes(s, jnp.maximum)
    for i in range(1, 4):

        @pl.when(x >= i)
        def _(i=i):
            for copy in copies(i):
                copy.wait()

    def first_pass(i, top):
        s = scores(buf[i, 0])
        s_ref[i] = s
        return jnp.maximum(top, lanes(s, jnp.maximum))

    top = lax.fori_loop(1, x + 1, first_pass, top)
    top = jnp.max(top, axis=1, keepdims=True)
    scale = HD**-0.5 * math.log2(math.e)

    def second_pass(i, state):
        tot, acc = state
        e = jnp.exp2((s_ref[i] - top) * scale)
        return tot + lanes(e, jnp.add), acc + jnp.dot(
            e.astype(jnp.bfloat16), buf[i, 1], preferred_element_type=jnp.float32
        )

    zero = jnp.zeros((rows, HD), jnp.float32)
    tot, acc = lax.fori_loop(0, x + 1, second_pass, (zero, zero))
    o_ref[...] = (acc / jnp.sum(tot, axis=1, keepdims=True)).astype(o_ref.dtype)


def project(info, h, pieces):
    count, m, part = h.shape
    hbm = pl.BlockSpec(memory_space=pl.ANY)
    return pl.pallas_call(
        project_kernel,
        in_specs=[pl.BlockSpec(memory_space=pltpu.SMEM)] + [hbm] * 5,
        out_specs=pl.BlockSpec(memory_space=pltpu.VMEM),
        out_shape=jax.ShapeDtypeStruct((2, m // 2, HD), jnp.float32),
        scratch_shapes=[
            pltpu.VMEM((4, count // 4, m, part), jnp.bfloat16),
            pltpu.VMEM((4, count // 4 * part, HD), jnp.bfloat16),
            pltpu.SemaphoreType.DMA((4, 5)),
        ],
        compiler_params=pltpu.CompilerParams(vmem_limit_bytes=48 * 2**20),
        cost_estimate=pl.CostEstimate(
            flops=2 * m * count * part * HD,
            bytes_accessed=2 * count * part * (m + HD),
            transcendentals=0,
        ),
        name="project",
    )(info, h, *pieces)


def attend(info, sums, cosine, sine, mine, other):
    vm = pl.BlockSpec(memory_space=pltpu.VMEM)
    return pl.pallas_call(
        attend_kernel,
        in_specs=[pl.BlockSpec(memory_space=pltpu.SMEM), vm, vm, vm]
        + [pl.BlockSpec(memory_space=pl.ANY)] * 6,
        out_specs=vm,
        out_shape=jax.ShapeDtypeStruct(sums.shape, jnp.bfloat16),
        scratch_shapes=[
            pltpu.VMEM((4, 2, 1536, HD), jnp.bfloat16),
            pltpu.VMEM((4, 192, 1536), jnp.float32),
            pltpu.SemaphoreType.DMA((4, 2)),
        ],
        compiler_params=pltpu.CompilerParams(vmem_limit_bytes=40 * 2**20),
        cost_estimate=pl.CostEstimate(
            flops=4 * 192 * 6144 * HD,
            bytes_accessed=4 * 6144 * HD,
            transcendentals=192 * 6144,
        ),
        name="attend",
    )(info, sums, cosine, sine, *mine, *other)


def shift(v, axis, by):
    n = lax.axis_size(axis)
    return lax.ppermute(v, axis, [(i, (i + by) % n) for i in range(n)])


def shift_up(v, axis, by):
    n = lax.axis_size(axis)
    return lax.ppermute(v, axis, [(i, i + by) for i in range(n - by)])


def swap(v, axis):
    return lax.ppermute(v, axis, [(0, 1), (1, 0)])


def body(hidden, query_weight, kv_weight):
    x, yq, yp, z, core = (lax.axis_index(a) for a in AXES)
    y = yq * 2 + yp
    base = (x * 8 + y) * 192
    info = jnp.stack([x, y, core])
    tie = lax.optimization_barrier

    (hs,) = small_kernel(slabs_kernel, "slabs", [(32, 12, 512)], (hidden,))
    hs, w = tie((hs, query_weight))
    hs = lax.all_to_all(hs, PAIR, 0, 0, tiled=True)

    one, three = shift(w, "yq", 1), shift(w, "yq", 3)
    hs, w, one, three = tie((hs, w, one, three))
    h, part = mix(info, hs, kv_weight)
    h = lax.all_gather(h, TP, axis=0, tiled=False)
    w = jnp.concatenate([w, one, shift(one, "yq", 1), three], axis=0)

    part = lax.all_to_all(part, PAIR, 0, 0, tiled=True)
    up, down = shift(w, "x", 1), shift(w, "x", -1)
    rows = jnp.sum(part, axis=0)
    cosine, sine = angles_of(base + z * 24 + jnp.arange(24, dtype=jnp.int32))
    rows = jnp.where(core == 0, rotate(rows, cosine, sine), rows).astype(jnp.bfloat16)
    rows = broadcast_gather(rows, ("yq", "yp", "z")).reshape(1536, HD)
    first, last = small_kernel(ends_kernel, "ends", [(1024, HD)] * 2, (up, down))
    cross = [shift(first, "x", 1), shift(last, "x", -1)]
    rows, cross = tie((rows, cross))
    mine = [rows] + [shift_up(rows, "x", d) for d in (1, 2, 3)]

    sums = project(info, h, (w, up, jnp.concatenate(cross, axis=0), down))
    keep = jnp.where(yp == 0, sums[0], sums[1])
    come = swap(jnp.where(yp == 0, sums[1], sums[0]), "yp")
    away, come = tie((mine[1:], come))
    (other,) = small_kernel(join_kernel, "join", [(4608, HD)], tuple(away))
    other = [swap(rows, "core"), swap(other, "core")]
    cosine, sine = angles_of(base + jnp.arange(192, dtype=jnp.int32))
    cosine = jnp.concatenate([cosine, cosine], axis=1)
    sine = jnp.concatenate([-sine, sine], axis=1)
    return attend(info, keep + come, cosine, sine, mine, other)


def solution(mesh):
    in_specs = (P(AXES, None), P(CTX, TP), P(TP, None))
    out_specs = P(CTX, TP)
    return jax.shard_map(
        body, mesh=fine_mesh(mesh), in_specs=in_specs, out_specs=out_specs, check_vma=False
    )
```
